512 devices in a mesh: grp: 16 (over z), dom: 32 (over y, x, core).
Axes of the slice: x: 4, y: 4, z: 16, core: 2. Of those that a mesh axis runs over, the one named last changes fastest.
Arguments:
- state: float32 [6, 125, 131072], P(None, None, ('grp', 'dom')), may hold values from -0.6 to 0.6
- adjoint: float32 [6, 125, 131072], P(None, None, ('grp', 'dom')), may hold values from -16 to 16
- factors: float32 [3, 5, 5, 131072], P(None, None, None, ('grp', 'dom')), may hold values from -3 to 3
- order: int32 [131072], P(('grp', 'dom')), may hold values from 1 to 4
- marks: int32 [131072], P(('grp', 'dom')), may hold values from -1 to 1
- neighbours: int32 [6, 131072], P(None, ('grp', 'dom')), may hold values from 0 to 255
- new_owner: int32 [131072, 1], P(('grp', 'dom')), may hold values from 0 to 15; in each aligned block of 256 rows (0 to 255, 256 to 511, ...) at most 24 rows name the same one
Outputs:
- share: float32 [131072], P(('grp', 'dom'))
- moved_state: float32 [6, 125, 196608], P(None, None, ('grp', 'dom'))
- moved_adjoint: float32 [6, 125, 196608], P(None, None, ('grp', 'dom'))
- moved_factors: float32 [3, 5, 5, 196608], P(None, None, None, ('grp', 'dom'))
- moved_order: int32 [196608], P(('grp', 'dom'))
The draws below stay inside these ranges and needn't reach their ends.
Inputs may be any that keep to these rules, and one draw needn't show every extreme that they name: `new_owner`: within each partition's 256 elements, no group index is named more than 24 times, and in every draw some group is named exactly 24 times by some partition.
All inputs are finite; a program needn't handle non-finite values.
Results may differ from the reference program's by a relative error of at most 0.0003.
Values sent between devices are 32-bit elements; how exact they have to be, the bound alone decides.
A program may use at most 128 MiB of HBM per device.

```python
import math
import jax
import jax.numpy as jnp
import numpy as np
from jax import lax

NV = 6
PMAX = 4
P1 = 5
MODES = 125
NQ1 = 7
ELEM_DEV = 256
CAP = 24
NELEM = 131072
N_GRP = 16
N_DOM = 32


def draw_adjoint(key, part):
    key = jax.random.fold_in(key, 7)
    place = jnp.arange(NELEM, dtype=jnp.float32) / NELEM
    raw = jnp.clip(jax.random.normal(key, (NV, MODES, NELEM), jnp.float32), -5.0, 5.0)
    return raw * (1.0 + 2.0 * place)[None, None, :]


def plant(drawn, key, smallest, high):
    dims = drawn.shape
    spot = [jax.random.randint(jax.random.fold_in(key, axis), (), 0, dims[axis]) for axis in range(len(dims))]
    drawn = drawn.at[tuple(spot)].set(smallest)
    longest = dims.index(max(dims))
    spot[longest] = (spot[longest] + 1) % dims[longest]
    return drawn.at[tuple(spot)].set(high)


def level_of(key, dims, pieces, low, high):
    def one(position, shards_of):
        draws = jax.random.uniform(jax.random.fold_in(jax.random.fold_in(key, 6), position), (shards_of,), jnp.float32, low / len(pieces), high / len(pieces))
        return jnp.repeat(jnp.exp(draws), dims[position] // shards_of).reshape((-1,) + (1,) * (len(dims) - position - 1))

    factor_of = one(*pieces[0])
    for cut in pieces[1:]:
        factor_of = factor_of * one(*cut)
    return factor_of


def shared_out(rng, own, number, rows, amount, top, reach, skew):
    ranking = jax.random.permutation(rng, amount)
    crowded, usual = portions_of(amount, rows * top, reach, skew, True), portions_of(amount, rows * top, reach, skew, False)
    places = jnp.arange(amount)

    def named(tallies, turn):
        used = int((tallies > 0).sum())
        fixed = max(1, used // 4)
        passed = fixed + (places - fixed + turn * (used - fixed)) % max(1, amount - fixed)
        return jnp.zeros((amount,), jnp.int32).at[ranking[jnp.where(places < fixed, places, passed)]].set(jnp.asarray(tallies, jnp.int32))

    tallies = jnp.where(number % 4 == 0, named(crowded, number // 4), named(usual, number - number // 4 - 1))
    mixed = jax.random.permutation(jax.random.fold_in(own, 3), amount)
    source_of, receiver = mixed[0:amount // 2 * 2:2], mixed[1:amount // 2 * 2:2]
    slack = jnp.minimum(tallies[source_of] - 1, reach - tallies[receiver]) // 2
    slack = jnp.where((source_of == ranking[0]) | (receiver == ranking[0]) | (tallies[receiver] == 0), 0, jnp.maximum(slack, 0))
    passed = jax.random.randint(jax.random.fold_in(own, 4), (amount // 2,), 0, 1 << 20) % (slack + 1)
    tallies = tallies.at[source_of].add(-passed).at[receiver].add(passed)
    labels = jnp.searchsorted(jnp.cumsum(tallies), jnp.arange(rows * top), side="right").astype(jnp.int32)
    listing = labels.reshape(top, rows).T
    listing = listing[jax.random.permutation(jax.random.fold_in(own, 1), rows)]
    turn = jax.random.randint(jax.random.fold_in(own, 2), (rows, 1), 0, top)
    return jnp.take_along_axis(listing, (jnp.arange(top)[None, :] + turn) % top, axis=1)


def portions_of(amount, total, reach, skew, full):
    loads = [(1 << 20) // math.isqrt(rank ** skew) + 1 for rank in range(1, amount + 1)]
    largest = reach if full else min(reach, max(-(-total // amount), total * loads[0] // sum(loads)))
    least = 1 if total - largest >= amount - 1 else 0
    given, rest = [largest] + [least] * (amount - 1), total - largest - least * (amount - 1)
    while rest > 0:
        candidates = [i for i in range(1, amount) if given[i] < largest] or [i for i in range(1, amount) if given[i] < reach]
        pool, left = sum([loads[i] for i in candidates]), rest
        for i in candidates:
            extra = min(reach - given[i], max(1, left * loads[i] // pool), rest)
            given[i] = given[i] + extra
            rest = rest - extra
    return np.array(given)


def gaussian(key, extent, scale, most, cuts=(), kind=jnp.bfloat16):
    loudness = level_of(key, extent, cuts, -0.22, 0.18) if cuts else 1.0
    entries = jax.random.normal(key, extent, jnp.float32) * scale * loudness
    return jnp.minimum(jnp.maximum(entries, -most), most).astype(kind)


def setup_inputs(seed: int = 0) -> dict:
    keys = jax.random.split(jax.random.key(seed), 8)
    state = gaussian(keys[0], (NV, MODES, NELEM), 0.1, 0.6, ((2, 512),), jnp.float32)
    adjoint = draw_adjoint(jax.random.fold_in(keys[7], 71), 0)
    factors = gaussian(keys[2], (3, P1, P1, NELEM), 0.5, 3.0, ((3, 512),), jnp.float32)
    order = plant(jax.random.randint(keys[3], (NELEM,), 1, PMAX + 1), jax.random.fold_in(keys[3], 1), 1, PMAX).astype(jnp.int32)
    marks = plant(jax.random.randint(keys[4], (NELEM,), -1, 2), jax.random.fold_in(keys[4], 1), -1, 1).astype(jnp.int32)
    neighbours = plant(jax.random.randint(keys[5], (6, NELEM), 0, ELEM_DEV), jax.random.fold_in(keys[5], 1), 0, ELEM_DEV - 1).astype(jnp.int32)
    new_owner_keys = jax.random.split(jax.random.fold_in(keys[6], 1), NELEM // ELEM_DEV)
    new_owner_turns = jax.random.permutation(jax.random.fold_in(keys[6], 3), NELEM // ELEM_DEV)
    new_owner = jax.vmap(lambda own, number: shared_out(jax.random.fold_in(keys[6], 2), own, number, ELEM_DEV, N_GRP, 1, CAP, 2))(new_owner_keys, new_owner_turns).reshape((NELEM, 1))
    return dict(state=state, adjoint=adjoint, factors=factors, order=order, marks=marks, neighbours=neighbours, new_owner=new_owner)


HIGH_ORDER_LEVEL = lax.Precision.HIGHEST

def legendre(count, points):
    values = [jnp.ones_like(points), points]
    slopes = [jnp.zeros_like(points), jnp.ones_like(points)]
    for level in range(1, count - 1):
        values.append(((2 * level + 1) * points * values[level] - level * values[level - 1]) / (level + 1))
        slopes.append(slopes[level - 1] + (2 * level + 1) * values[level])
    value_tab = jnp.stack([values[level] * math.sqrt((2 * level + 1) / 2.0) for level in range(count)])
    slope_tab = jnp.stack([slopes[level] * math.sqrt((2 * level + 1) / 2.0) for level in range(count)])
    return (value_tab, slope_tab)

def tables(line, points_line):
    angle = math.pi * (jnp.arange(points_line, dtype=jnp.float32) + 0.5) / points_line
    points = -jnp.cos(angle)
    weights = math.pi / points_line * jnp.sin(angle)
    value_tab, slope_tab = legendre(line, points)
    vt = value_tab.T
    st = slope_tab.T
    minus_end = jnp.array([math.sqrt((2 * n + 1) / 2.0) * (-1.0) ** n for n in range(line)], jnp.float32)
    plus_end = jnp.array([math.sqrt((2 * n + 1) / 2.0) for n in range(line)], jnp.float32)
    count = line ** 3
    npts = points_line ** 3

    def volume(first, second, third):
        prod = first[:, None, None, :, None, None] * second[None, :, None, None, :, None] * third[None, None, :, None, None, :]
        return prod.reshape(npts, count)
    basis = volume(vt, vt, vt)
    wvol = (weights[:, None, None] * weights[None, :, None] * weights[None, None, :]).reshape(npts)
    grads = [volume(st, vt, vt), volume(vt, st, vt), volume(vt, vt, st)]
    check_cases = [grad * wvol[:, None] for grad in grads]
    wface = (weights[:, None] * weights[None, :]).reshape(points_line * points_line)
    element_faces = []
    for sweep_direction in range(3):
        for ends in (minus_end, plus_end):
            if sweep_direction == 0:
                prod = ends[None, None, :, None, None] * vt[:, None, None, :, None] * vt[None, :, None, None, :]
            elif sweep_direction == 1:
                prod = vt[:, None, :, None, None] * ends[None, None, None, :, None] * vt[None, :, None, None, :]
            else:
                prod = vt[:, None, :, None, None] * vt[None, :, None, :, None] * ends[None, None, None, None, :]
            element_faces.append(prod.reshape(points_line * points_line, count))
    index = jnp.arange(count, dtype=jnp.int32)
    top = jnp.maximum(jnp.maximum(index // (line * line), index // line % line), index % line)
    return (basis, grads, check_cases, element_faces, wface, top)

def contract(lookup_table, solution_field):
    return jnp.einsum('hn,anq->ahq', lookup_table, solution_field, precision=HIGH_ORDER_LEVEL)

def speeds(solution_field, sweep_direction):
    return solution_field[1 + sweep_direction] / jnp.sqrt(1.0 + solution_field[0] * solution_field[0])

def face_flux(inner, outer, sweep_direction, side):
    sign = 2.0 * side - 1.0
    carried = speeds(inner, sweep_direction)[None] * inner + speeds(outer, sweep_direction)[None] * outer
    return 0.5 * sign * carried + 0.5 * (inner - outer)

def residual(state_p, own, outside, basis, grads, check_cases, element_faces, wface):
    values = contract(basis, state_p)
    viscous = 0.05 + 0.1 * jax.nn.softplus(values[5])
    grand_total = jnp.zeros(state_p.shape, jnp.float32)
    for sweep_direction in range(3):
        slope = contract(grads[sweep_direction], state_p)
        numerical_flux = speeds(values, sweep_direction)[None] * values - viscous[None] * slope
        grand_total = grand_total - jnp.einsum('to,ytn->yon', check_cases[sweep_direction], numerical_flux, precision=HIGH_ORDER_LEVEL)
    for element_face in range(6):
        numerical_flux = face_flux(own[element_face], outside[element_face], element_face // 2, element_face % 2) * wface[None, :, None]
        grand_total = grand_total + jnp.einsum('ty,jtb->jyb', element_faces[element_face], numerical_flux, precision=HIGH_ORDER_LEVEL)
    return grand_total

def reference(state, adjoint, factors, order, marks, neighbours, new_owner):
    basis, grads, check_cases, element_faces, wface, top = tables(P1, NQ1)
    groups = N_GRP
    doms = N_DOM
    devs = groups * doms
    elems = ELEM_DEV
    keep_p = (top[:, None] <= order[None, :]).astype(jnp.float32)
    keep_q = (top[:, None] <= (order + 1)[None, :]).astype(jnp.float32)
    state_p = state * keep_p[None]
    psi = adjoint * keep_q[None]

    def to_blocks(solution_field):
        return solution_field.reshape(solution_field.shape[0], solution_field.shape[1], devs, elems).transpose(2, 0, 1, 3)
    state_blocks = to_blocks(state_p)
    psi_blocks = to_blocks(psi)
    nbr_blocks = neighbours.reshape(6, devs, elems).transpose(1, 0, 2)

    def end_traces(block):
        return (contract(element_faces[4], block), contract(element_faces[5], block))
    minus_all, plus_all = lax.map(end_traces, state_blocks)
    nf = minus_all.shape[2]
    plus_grid = plus_all.reshape(groups, doms, NV, nf, elems)
    minus_grid = minus_all.reshape(groups, doms, NV, nf, elems)
    zero_row = jnp.zeros((groups, 1, NV, nf, elems), jnp.float32)
    lower_plus = jnp.concatenate([zero_row, plus_grid[:, :-1]], axis=1).reshape(devs, NV, nf, elems)
    upper_minus = jnp.concatenate([minus_grid[:, 1:], zero_row], axis=1).reshape(devs, NV, nf, elems)

    def one_device(items):
        block, psi_block, nbr, lower, upper = items
        own = [contract(element_faces[element_face], block) for element_face in range(6)]
        outside = [jnp.take(own[1], nbr[0], axis=2), jnp.take(own[0], nbr[1], axis=2), jnp.take(own[3], nbr[2], axis=2), jnp.take(own[2], nbr[3], axis=2), jnp.take(lower, nbr[4], axis=2), jnp.take(upper, nbr[5], axis=2)]
        result = residual(block, own, outside, basis, grads, check_cases, element_faces, wface)
        return jnp.abs(lax.optimization_barrier(jnp.sum(psi_block * result, axis=(0, 1))))
    eta = lax.map(one_device, (state_blocks, psi_blocks, nbr_blocks, lower_plus, upper_minus)).reshape(devs * elems)
    share = eta / (jnp.mean(eta) + 1e-06)
    new_order = jnp.clip(order + marks, 1, PMAX)
    low = jnp.minimum(order, new_order)
    move_state = state * (top[:, None] <= low[None, :]).astype(jnp.float32)[None]
    move_adjoint = adjoint * (top[:, None] <= new_order[None, :]).astype(jnp.float32)[None]
    line = (jnp.arange(P1, dtype=jnp.int32)[:, None] <= low[None, :]).astype(jnp.float32)
    move_factors = factors * (line[:, None, :] * line[None, :, :])[None]
    dest = new_owner[:, 0].reshape(devs, elems)
    onehot = (dest[:, :, None] == jnp.arange(groups, dtype=jnp.int32)[None, None, :]).astype(jnp.int32)
    rank = lax.optimization_barrier(jnp.sum((jnp.cumsum(onehot, axis=1) - onehot) * onehot, axis=2))
    device = jnp.arange(devs, dtype=jnp.int32)[:, None]
    source_grp = device // doms
    source_dom = device % doms
    gslot = (((dest * doms + source_dom) * groups + source_grp) * CAP + rank).reshape(devs * elems)
    slots = devs * groups * CAP
    moved_state = jnp.zeros((NV, MODES, slots), jnp.float32).at[:, :, gslot].set(move_state)
    moved_adjoint = jnp.zeros((NV, MODES, slots), jnp.float32).at[:, :, gslot].set(move_adjoint)
    moved_factors = jnp.zeros((3, P1, P1, slots), jnp.float32).at[:, :, :, gslot].set(move_factors)
    moved_order = jnp.zeros((slots,), jnp.int32).at[gslot].set(new_order.astype(jnp.int32))
    return (share, moved_state, moved_adjoint, moved_factors, moved_order)
```

```python
import functools
import math

import jax
import jax.numpy as jnp
import ml_dtypes
import numpy as np
from jax import lax
from jax.experimental import pallas as pl
from jax.experimental.pallas import tpu as pltpu
from jax.sharding import PartitionSpec as P

NV = 6
PMAX = 4
P1 = 5
MODES = 125
NQ1 = 7
ELEM = 256
CAP = 24
GRP = 16
DOM = 32
SLOTS = GRP * CAP
LEAF = 8
ROWS = DOM // LEAF
MPAD = 128
PT = 56
TM = 32
KCAT = 3 * MPAD
FROWS = 3 * P1 * P1 + 1
SPARE = MPAD - MODES
REST = FROWS - 2 * NV * SPARE
REST_AT = 2 * NV * SPARE % 8
MESH = pl.DeviceIdType.MESH
CHUNKS = ((0, 1), (1, 3), (4, 4), (8, 4))
F32 = jnp.float32
BF16 = jnp.bfloat16


def line_tables():
    place = math.pi * (np.arange(NQ1) + 0.5) / NQ1
    points = -np.cos(place)
    weights = math.pi / NQ1 * np.sin(place)
    values = [np.ones(NQ1), points]
    slopes = [np.zeros(NQ1), np.ones(NQ1)]
    for n in range(1, P1 - 1):
        values.append(((2 * n + 1) * points * values[n] - n * values[n - 1]) / (n + 1))
        slopes.append(slopes[n - 1] + (2 * n + 1) * values[n])
    norm = np.sqrt((2 * np.arange(P1) + 1) / 2.0)
    vt = np.stack(values, axis=1) * norm
    st = np.stack(slopes, axis=1) * norm
    ends = [norm * (-1.0) ** np.arange(P1), norm]
    return vt, st, ends, weights


def split(table):
    high = table.astype(np.float32).astype(ml_dtypes.bfloat16)
    low = (table - high.astype(np.float64)).astype(np.float32).astype(ml_dtypes.bfloat16)
    return high, low


def against_split(table):
    rows, depth = table.shape
    pad = MPAD if depth == MODES else TM
    high, low = split(table)
    out = np.zeros((rows, 3 * pad), ml_dtypes.bfloat16)
    out[:, :depth] = high
    out[:, pad : pad + depth] = high
    out[:, 2 * pad : 2 * pad + depth] = low
    return out


def padded(table, rows):
    return np.concatenate([table, np.zeros((rows - table.shape[0],) + table.shape[1:])])


def tables():
    vt, st, ends, w = line_tables()

    def plane(a, first, second, third):
        return np.einsum("i,bj,ck->bcijk", first[a], second, third).reshape(NQ1 * NQ1, MODES)

    face_w = np.outer(w, w).reshape(-1, 1)
    vol_u, vol_p = [], []
    for a in range(NQ1):
        grads = [plane(a, st, vt, vt), plane(a, vt, st, vt), plane(a, vt, vt, st)]
        vol_u.append(np.concatenate([padded(t, PT) for t in [plane(a, vt, vt, vt)] + grads]))
        vol_p.append(padded(np.concatenate([padded(w[a] * face_w * t, PT) for t in grads]), 176))
    eye = np.eye(P1)

    def face(f, tangent):
        e = ends[f % 2][None]
        parts = [e, tangent, tangent] if f < 2 else [tangent, e, tangent] if f < 4 else [tangent, tangent, e]
        out = np.einsum("ai,bj,ck->abcijk", *parts)
        return out.reshape(-1, MODES)

    modal = [padded(face(f, eye), TM) for f in (1, 0, 3, 2, 5, 4)]
    at_points = [padded(face(f, vt), PT) for f in range(6)]
    weighted = [padded(face_w * face(f, vt), PT) for f in range(6)]
    face_u = np.concatenate(modal + at_points)
    face_p = np.concatenate(weighted)
    tangents = padded(np.einsum("bj,ck->bcjk", vt, vt).reshape(NQ1 * NQ1, P1 * P1), 64)
    return (
        np.stack([against_split(t) for t in vol_u]),
        np.stack([against_split(t) for t in vol_p]),
        against_split(face_u),
        against_split(face_p),
        against_split(tangents),
    )


def dot(a, b):
    return lax.dot_general(a, b, (((1,), (0,)), ((), ())), preferred_element_type=F32)


def dot_rows(a, b):
    return lax.dot_general(a, b, (((1,), (1,)), ((), ())), preferred_element_type=F32)


def halves(x):
    high = x.astype(BF16)
    return high, (x - high.astype(F32)).astype(BF16)


def thirds(x):
    high = x.astype(BF16)
    rest = x - high.astype(F32)
    mid = rest.astype(BF16)
    return high, mid, (rest - mid.astype(F32)).astype(BF16)


def digit_sum(m, step, count):
    total = jnp.zeros(m.shape, jnp.int32)
    for n in range(1, count):
        total = total + jnp.where(m >= n * step, 1, 0)
    return total


def top_of(rows):
    m = lax.broadcasted_iota(jnp.int32, (rows, ELEM), 0)
    i = digit_sum(m, P1 * P1, P1)
    m = m - i * (P1 * P1)
    j = digit_sum(m, P1, P1)
    k = m - j * P1
    return jnp.maximum(jnp.maximum(i, j), k)


def factor_top(rows):
    m = lax.broadcasted_iota(jnp.int32, (rows, ELEM), 0)
    d = digit_sum(m, P1 * P1, 3)
    m = m - d * (P1 * P1)
    i = digit_sum(m, P1, P1)
    j = m - i * P1
    return jnp.maximum(i, j)


def speed(values, lead):
    return lead * lax.rsqrt(1.0 + values * values)


def work(
    state,
    adjoint_hbm,
    factors,
    order,
    marks,
    neighbours,
    owner,
    vol_u_hbm,
    vol_p_hbm,
    face_u_hbm,
    face_p_hbm,
    tangents,
    recv,
    recv_rest,
    share,
    adjoint,
    vol_u,
    vol_p,
    face_u,
    face_p,
    send,
    send_rest,
    sel,
    top,
    padded_x,
    fac,
    fac3,
    us,
    ps,
    hsend,
    outer,
    own,
    own_p,
    vals,
    vals_p,
    near,
    gath,
    leaf_sum,
    row_sum,
    grp_sum,
    load_sem,
    self_sem,
    send_sem,
    recv_sem,
    halo_send,
    halo_recv,
    leaf_send,
    leaf_recv,
    row_send,
    row_recv,
    sum_send,
    sum_recv,
):
    g = lax.axis_index("grp")
    r = lax.axis_index("dom")
    lane = lax.rem(r, LEAF)
    row = r // LEAF
    after = lax.rem(r + 1, DOM)
    before = lax.rem(r + DOM - 1, DOM)

    barrier = pltpu.get_barrier_semaphore()

    def greet(to_g, to_r):
        pl.semaphore_signal(barrier, inc=1, device_id=(to_g, to_r), device_id_type=MESH)

    @pl.loop(1, GRP)
    def _(k):
        greet(lax.rem(g + k, GRP), r)

    @pl.loop(1, LEAF)
    def _(k):
        greet(g, row * LEAF + lax.rem(lane + k, LEAF))

    @pl.loop(1, ROWS)
    def _(k):
        greet(g, lax.rem(row + k, ROWS) * LEAF + lane)

    greet(g, after)
    greet(g, before)
    greeted = GRP + LEAF + ROWS - 1

    loads = [
        pltpu.make_async_copy(source, target, load_sem.at[n])
        for n, (source, target) in enumerate(
            (
                (adjoint_hbm, adjoint),
                (face_u_hbm, face_u),
                (vol_u_hbm, vol_u),
                (vol_p_hbm, vol_p),
                (face_p_hbm, face_p),
            )
        )
    ]
    for load in loads:
        load.start()

    to = owner[...]
    hits = jnp.where(lax.broadcasted_iota(jnp.int32, (GRP, ELEM), 0) == to, 1.0, 0.0)
    earlier = jnp.where(
        lax.broadcasted_iota(jnp.int32, (ELEM, ELEM), 0)
        < lax.broadcasted_iota(jnp.int32, (ELEM, ELEM), 1),
        1.0,
        0.0,
    ).astype(BF16)
    counts = dot(hits.astype(BF16), earlier)
    rank = jnp.sum(hits * counts, axis=0, keepdims=True).astype(jnp.int32)
    slot = to * CAP + rank
    sel[...] = jnp.where(
        lax.broadcasted_iota(jnp.int32, (SLOTS, ELEM), 0) == slot, 1.0, 0.0
    ).astype(BF16)

    level = order[...]
    fresh = jnp.clip(level + marks[...], 1, PMAX)
    low = jnp.minimum(level, fresh)
    top[...] = top_of(MPAD)

    for d in range(3):
        for i in range(P1):
            at = (d * P1 + i) * P1
            fac[at : at + P1, :] = factors[d, i]
    fac[FROWS - 1 : 80, :] = jnp.zeros((80 - FROWS + 1, ELEM), F32)
    rows = lax.broadcasted_iota(jnp.int32, (80, ELEM), 0)
    kept = jnp.where(factor_top(80) <= low, fac[...], 0.0)
    fac[...] = jnp.where(rows == FROWS - 1, fresh.astype(F32), kept)
    for n in range(2 * NV):
        fac3[n, 0:SPARE, :] = fac[n * SPARE : (n + 1) * SPARE, :]

    def pack(source, v, most, column):
        padded_x[0:MODES, :] = jnp.where(top[0:MODES, :] <= most, source[v], 0.0)
        padded_x[MODES:MPAD, :] = fac3[column, 0:SPARE, :]
        high, mid, tail = thirds(padded_x[...])
        chosen = sel[...]
        send[column] = dot_rows(chosen, high) + dot_rows(chosen, mid) + dot_rows(chosen, tail)

    def copy_to(c, j):
        first, count = CHUNKS[c]
        ahead = lax.rem(j, 2) * ((j + 1) // 2) + (1 - lax.rem(j, 2)) * (GRP - j // 2)
        to_g = lax.rem(g + ahead, GRP)
        return pltpu.make_async_remote_copy(
            src_ref=send.at[pl.ds(first, count), pl.ds(to_g * CAP, CAP)],
            dst_ref=recv.at[pl.ds(first, count), pl.ds(g * CAP, CAP)],
            send_sem=send_sem.at[c, j],
            recv_sem=recv_sem.at[c, j],
            device_id=(to_g, r),
            device_id_type=MESH,
        )

    def rest_to(j):
        ahead = lax.rem(j, 2) * ((j + 1) // 2) + (1 - lax.rem(j, 2)) * (GRP - j // 2)
        to_g = lax.rem(g + ahead, GRP)
        return pltpu.make_async_remote_copy(
            src_ref=send_rest.at[pl.ds(to_g * 8, 8)],
            dst_ref=recv_rest.at[pl.ds(g * 8, 8)],
            send_sem=send_sem.at[len(CHUNKS), j],
            recv_sem=recv_sem.at[len(CHUNKS), j],
            device_id=(to_g, r),
            device_id_type=MESH,
        )

    def self_copy(c):
        first, count = CHUNKS[c]
        return pltpu.make_async_copy(
            send.at[pl.ds(first, count), pl.ds(g * CAP, CAP)],
            recv.at[pl.ds(first, count), pl.ds(g * CAP, CAP)],
            self_sem.at[c],
        )

    def self_rest():
        return pltpu.make_async_copy(
            send_rest.at[pl.ds(g * 8, 8)], recv_rest.at[pl.ds(g * 8, 8)], self_sem.at[len(CHUNKS)]
        )

    def send_chunk(c):
        @pl.loop(1, GRP)
        def _(j):
            copy_to(c, j).start()

        self_copy(c).start()

    pack(state, 0, low, 0)
    pl.semaphore_wait(barrier, greeted)
    send_chunk(0)

    def split_into(target, source, v, most):
        padded_x[0:MODES, :] = jnp.where(top[0:MODES, :] <= most, source[v], 0.0)
        padded_x[MODES:MPAD, :] = jnp.zeros((SPARE, ELEM), F32)
        high, tail = halves(padded_x[...])
        target[v, 0:MPAD, :] = high
        target[v, MPAD : 2 * MPAD, :] = tail
        target[v, 2 * MPAD :, :] = high

    loads[1].wait()

    @pl.loop(0, NV)
    def _(v):
        split_into(us, state, v, level)
        both = dot(face_u[...], us[v])
        place = pl.ds(pl.multiple_of(v * TM, TM), TM)
        for b in range(4):
            outer[b, place, :] = both[b * TM : (b + 1) * TM]
        hsend[0, place, :] = both[4 * TM : 5 * TM]
        hsend[1, place, :] = both[5 * TM : 6 * TM]
        for f in range(6):
            own[f, v] = both[6 * TM + f * PT : 6 * TM + (f + 1) * PT]

    halos = [
        pltpu.make_async_remote_copy(
            src_ref=hsend.at[n],
            dst_ref=outer.at[4 + n],
            send_sem=halo_send.at[n],
            recv_sem=halo_recv.at[n],
            device_id=(g, to_r),
            device_id_type=MESH,
        )
        for n, to_r in enumerate((after, before))
    ]
    for halo in halos:
        halo.start()

    @pl.loop(1, 4)
    def _(v):
        pack(state, v, low, v)

    send_chunk(1)
    loads[0].wait()

    @pl.loop(4, NV)
    def _(v):
        pack(state, v, low, v)

    @pl.loop(0, 2)
    def _(v):
        pack(adjoint, v, fresh, v + NV)

    send_chunk(2)

    @pl.loop(2, NV)
    def _(v):
        pack(adjoint, v, fresh, v + NV)

    total_rest = jnp.zeros((GRP * 8, MPAD), F32)
    line = lax.broadcasted_iota(jnp.int32, (GRP * 8, ELEM), 0)
    line_slot = (line // 8) * CAP + lax.rem(line, 8)
    from_row = 2 * NV * SPARE - REST_AT
    rest = fac[from_row : from_row + REST + 8, :]
    rest = jnp.concatenate([rest, jnp.zeros((MPAD - REST - 8, ELEM), F32)], axis=0)
    rest = jnp.where(lax.broadcasted_iota(jnp.int32, (MPAD, ELEM), 0) < REST_AT, 0.0, rest)
    for part in range(3):
        chosen = jnp.where(line_slot + 8 * part == slot, 1.0, 0.0).astype(BF16)
        moved = rest if part == 0 else pltpu.roll(rest, REST * part, 0)
        for piece in thirds(moved):
            total_rest = total_rest + dot_rows(chosen, piece)
    send_rest[...] = total_rest

    @pl.loop(1, GRP)
    def _(j):
        rest_to(j).start()

    self_rest().start()
    send_chunk(3)

    @pl.loop(0, NV)
    def _(v):
        split_into(ps, adjoint, v, level + 1)

    loads[2].wait()
    loads[3].wait()
    near[...] = jnp.zeros(near.shape, F32)

    @pl.loop(0, NQ1)
    def _(a):
        @pl.loop(0, NV)
        def _(v):
            vals[v] = dot(vol_u[a], us[v])
            vals_p[v] = dot(vol_p[a], ps[v])

        @pl.loop(0, PT // 8)
        def _(t):
            def at(table, v):
                return vals[v, pl.ds(pl.multiple_of(table * PT + t * 8, 8), 8), :]

            def at_p(table, v):
                return vals_p[v, pl.ds(pl.multiple_of(table * PT + t * 8, 8), 8), :]

            u0 = at(0, 0)
            inverse = lax.rsqrt(1.0 + u0 * u0)
            c = [at(0, 1 + d) * inverse for d in range(3)]
            u5 = at(0, 5)
            soft = jnp.maximum(u5, 0.0) + jnp.log1p(jnp.exp(-jnp.abs(u5)))
            nu = 0.05 + 0.1 * soft
            total = jnp.zeros((8, ELEM), F32)
            for v in range(NV):
                w = [at_p(d, v) for d in range(3)]
                carried = w[0] * c[0] + w[1] * c[1] + w[2] * c[2]
                spread = w[0] * at(1, v) + w[1] * at(2, v) + w[2] * at(3, v)
                total = total + (carried * at(0, v) - nu * spread)
            near[...] = near[...] - total

    loads[4].wait()

    @pl.loop(0, NV)
    def _(v):
        both = dot(face_p[...], ps[v])
        for f in range(6):
            own_p[f, v] = both[f * PT : (f + 1) * PT]

    for halo in halos:
        halo.wait()

    @pl.loop(0, 6)
    def _(f):
        absent = jnp.where(f == 4, jnp.where(r == 0, 1, 0), 0) + jnp.where(
            f == 5, jnp.where(r == DOM - 1, 1, 0), 0
        )
        present = 1.0 - absent.astype(F32)
        high, tail = halves(outer[f] * present)
        source = lax.broadcasted_iota(jnp.int32, (ELEM, ELEM), 0)
        pick = jnp.where(source == neighbours[pl.ds(f, 1), :], 1.0, 0.0).astype(BF16)
        got_high = dot(high, pick).astype(BF16)
        got_tail = dot(tail, pick).astype(BF16)
        for v in range(NV):
            lanes = slice(v * ELEM, (v + 1) * ELEM)
            gath[0:TM, lanes] = got_high[v * TM : (v + 1) * TM]
            gath[TM : 2 * TM, lanes] = got_tail[v * TM : (v + 1) * TM]
            gath[2 * TM :, lanes] = got_high[v * TM : (v + 1) * TM]
        seen = dot(tangents[...], gath[...])
        o = [seen[0:PT, v * ELEM : (v + 1) * ELEM] for v in range(NV)]
        d = f // 2
        sign = (2 * lax.rem(f, 2) - 1).astype(F32)
        lead_o = jnp.where(d == 0, o[1], jnp.where(d == 1, o[2], o[3]))
        half = 0.5 * sign
        speed_t = half * speed(own[f, 0], own[f, 1 + d])
        speed_o = half * speed(o[0], lead_o)
        total = jnp.zeros((PT, ELEM), F32)
        for v in range(NV):
            t = own[f, v]
            total = total + own_p[f, v] * (
                speed_t * t + speed_o * o[v] + 0.5 * (t - o[v])
            )
        part = total[0:8]
        for n in range(1, PT // 8):
            part = part + total[n * 8 : (n + 1) * 8]
        near[...] = near[...] + part

    eta = jnp.abs(jnp.sum(near[...], axis=0, keepdims=True))

    def exchange(buffer, mine, count, send_s, recv_s, device):
        def one(k):
            return pltpu.make_async_remote_copy(
                src_ref=buffer.at[mine],
                dst_ref=buffer.at[mine],
                send_sem=send_s.at[k],
                recv_sem=recv_s.at[k],
                device_id=device(k),
                device_id_type=MESH,
            )

        @pl.loop(1, count)
        def _(k):
            one(k).start()

        @pl.loop(1, count)
        def _(k):
            one(k).wait()

        return jnp.sum(buffer[...], axis=0)

    leaf_sum[lane] = jnp.broadcast_to(jnp.sum(eta, axis=1, keepdims=True), (8, 128))
    part = exchange(
        leaf_sum, lane, LEAF, leaf_send, leaf_recv,
        lambda k: (g, row * LEAF + lax.rem(lane + k, LEAF)),
    )
    row_sum[row] = part
    part = exchange(
        row_sum, row, ROWS, row_send, row_recv,
        lambda k: (g, lax.rem(row + k, ROWS) * LEAF + lane),
    )
    grp_sum[g] = part
    part = exchange(
        grp_sum, g, GRP, sum_send, sum_recv, lambda k: (lax.rem(g + k, GRP), r)
    )
    mean = part[0:1, 0:1] / (ELEM * GRP * DOM)
    share[...] = eta / (mean + 1e-06)

    for c in range(len(CHUNKS)):
        self_copy(c).wait()

        @pl.loop(1, GRP)
        def _(j):
            copy_to(c, j).wait()

    self_rest().wait()

    @pl.loop(1, GRP)
    def _(j):
        rest_to(j).wait()


def unpack(cols_s, cols_p, rest, share_in, moved_state, moved_adjoint, moved_factors, moved_order, share, fac):
    v = pl.program_id(0)
    first = cols_s[0].T
    second = cols_p[0].T
    moved_state[0] = first[0:MODES]
    moved_adjoint[0] = second[0:MODES]
    fac[v, 0:SPARE, :] = first[MODES:MPAD]
    fac[NV + v, 0:SPARE, :] = second[MODES:MPAD]

    @pl.when(v == NV - 1)
    def _():
        lines = rest[...].reshape(GRP, 1, 8, MPAD)
        parts = [lines] + [
            pltpu.roll(rest[...], MPAD - REST * n, 1).reshape(GRP, 1, 8, MPAD) for n in (1, 2)
        ]
        tail = jnp.concatenate(parts, axis=1).reshape(SLOTS, MPAD).T
        rows = [fac[n, 0:SPARE, :] for n in range(2 * NV)] + [tail[REST_AT : REST_AT + REST]]
        whole = jnp.concatenate(rows, axis=0)
        for d in range(3):
            for i in range(P1):
                at = (d * P1 + i) * P1
                moved_factors[d, i] = whole[at : at + P1]
        moved_order[...] = whole[FROWS - 1 : FROWS].astype(jnp.int32)
        share[...] = share_in[...]


def body(state, adjoint, factors, order, marks, neighbours, new_owner):
    vol_u, vol_p, face_u, face_p, tangents = [jnp.asarray(t) for t in tables()]
    vmem = pl.BlockSpec(memory_space=pltpu.VMEM)
    anywhere = pl.BlockSpec(memory_space=pl.ANY)
    dma = pltpu.SemaphoreType.DMA
    chunks = len(CHUNKS) + 1
    recv, recv_rest, share = pl.pallas_call(
        work,
        name="indicator_and_send",
        out_shape=(
            jax.ShapeDtypeStruct((2 * NV, SLOTS, MPAD), F32),
            jax.ShapeDtypeStruct((GRP * 8, MPAD), F32),
            jax.ShapeDtypeStruct((1, ELEM), F32),
        ),
        in_specs=[vmem, anywhere, vmem, vmem, vmem, vmem, vmem]
        + [anywhere] * 4
        + [vmem],
        out_specs=(anywhere, anywhere, vmem),
        scratch_shapes=[
            pltpu.VMEM((NV, MODES, ELEM), F32),
            pltpu.VMEM(vol_u.shape, BF16),
            pltpu.VMEM(vol_p.shape, BF16),
            pltpu.VMEM(face_u.shape, BF16),
            pltpu.VMEM(face_p.shape, BF16),
            pltpu.VMEM((2 * NV, SLOTS, MPAD), F32),
            pltpu.VMEM((GRP * 8, MPAD), F32),
            pltpu.VMEM((SLOTS, ELEM), BF16),
            pltpu.VMEM((MPAD, ELEM), jnp.int32),
            pltpu.VMEM((MPAD, ELEM), F32),
            pltpu.VMEM((80, ELEM), F32),
            pltpu.VMEM((2 * NV, 8, ELEM), F32),
            pltpu.VMEM((NV, KCAT, ELEM), BF16),
            pltpu.VMEM((NV, KCAT, ELEM), BF16),
            pltpu.VMEM((2, NV * TM, ELEM), F32),
            pltpu.VMEM((6, NV * TM, ELEM), F32),
            pltpu.VMEM((6, NV, PT, ELEM), F32),
            pltpu.VMEM((6, NV, PT, ELEM), F32),
            pltpu.VMEM((NV, 4 * PT, ELEM), F32),
            pltpu.VMEM((NV, 176, ELEM), F32),
            pltpu.VMEM((8, ELEM), F32),
            pltpu.VMEM((3 * TM, NV * ELEM), BF16),
            pltpu.VMEM((LEAF, 8, 128), F32),
            pltpu.VMEM((ROWS, 8, 128), F32),
            pltpu.VMEM((GRP, 8, 128), F32),
            dma((5,)),
            dma((chunks,)),
            dma((chunks, GRP)),
            dma((chunks, GRP)),
            dma((2,)),
            dma((2,)),
            dma((LEAF,)),
            dma((LEAF,)),
            dma((ROWS,)),
            dma((ROWS,)),
            dma((GRP,)),
            dma((GRP,)),
        ],
        compiler_params=pltpu.CompilerParams(
            collective_id=0, has_side_effects=True, vmem_limit_bytes=48 << 20
        ),
    )(
        state,
        adjoint,
        factors,
        order.reshape(1, ELEM),
        marks.reshape(1, ELEM),
        neighbours,
        new_owner.reshape(1, ELEM),
        vol_u,
        vol_p,
        face_u,
        face_p,
        tangents,
    )
    moved_state, moved_adjoint, moved_factors, moved_order, share = pl.pallas_call(
        unpack,
        name="unpack_slots",
        grid=(NV,),
        out_shape=(
            jax.ShapeDtypeStruct((NV, MODES, SLOTS), F32),
            jax.ShapeDtypeStruct((NV, MODES, SLOTS), F32),
            jax.ShapeDtypeStruct((3, P1, P1, SLOTS), F32),
            jax.ShapeDtypeStruct((1, SLOTS), jnp.int32),
            jax.ShapeDtypeStruct((1, ELEM), F32),
        ),
        in_specs=[
            pl.BlockSpec((1, SLOTS, MPAD), lambda v: (v, 0, 0)),
            pl.BlockSpec((1, SLOTS, MPAD), lambda v: (v + NV, 0, 0)),
            pl.BlockSpec((GRP * 8, MPAD), lambda v: (0, 0)),
            pl.BlockSpec((1, ELEM), lambda v: (0, 0)),
        ],
        out_specs=(
            pl.BlockSpec((1, MODES, SLOTS), lambda v: (v, 0, 0)),
            pl.BlockSpec((1, MODES, SLOTS), lambda v: (v, 0, 0)),
            pl.BlockSpec((3, P1, P1, SLOTS), lambda v: (0, 0, 0, 0)),
            pl.BlockSpec((1, SLOTS), lambda v: (0, 0)),
            pl.BlockSpec((1, ELEM), lambda v: (0, 0)),
        ),
        scratch_shapes=[pltpu.VMEM((2 * NV, 8, SLOTS), F32)],
        compiler_params=pltpu.CompilerParams(vmem_limit_bytes=16 << 20),
    )(recv, recv, recv_rest, share)
    return (
        share.reshape(ELEM),
        moved_state,
        moved_adjoint,
        moved_factors,
        moved_order.reshape(SLOTS),
    )


def solution(mesh):
    return jax.shard_map(
        body,
        mesh=mesh,
        in_specs=(
            P(None, None, ("grp", "dom")),
            P(None, None, ("grp", "dom")),
            P(None, None, None, ("grp", "dom")),
            P(("grp", "dom")),
            P(("grp", "dom")),
            P(None, ("grp", "dom")),
            P(("grp", "dom"), None),
        ),
        out_specs=(
            P(("grp", "dom")),
            P(None, None, ("grp", "dom")),
            P(None, None, ("grp", "dom")),
            P(None, None, None, ("grp", "dom")),
            P(("grp", "dom")),
        ),
        check_vma=False,
    )
```

```python
import functools
import math

import jax
import jax.numpy as jnp
import ml_dtypes
import numpy as np
from jax import lax
from jax.experimental import pallas as pl
from jax.experimental.pallas import tpu as pltpu
from jax.sharding import PartitionSpec as P

NV = 6
PMAX = 4
P1 = 5
MODES = 125
NQ1 = 7
ELEM = 256
CAP = 24
GRP = 16
DOM = 32
SLOTS = GRP * CAP
LEAF = 8
ROWS = DOM // LEAF
MPAD = 128
PT = 56
TM = 32
KCAT = 3 * MPAD
FROWS = 3 * P1 * P1 + 1
SPARE = MPAD - MODES
REST = FROWS - 2 * NV * SPARE
REST_AT = 2 * NV * SPARE % 8
MESH = pl.DeviceIdType.MESH
COLS = 2 * NV
BLOCK = COLS * CAP + 8
PIECES = ((0, 1), (1, 2), (3, 3), (6, 3), (9, 3))
NEAR = 2
BEFORE = 4
F32 = jnp.float32
BF16 = jnp.bfloat16


def line_tables():
    place = math.pi * (np.arange(NQ1) + 0.5) / NQ1
    points = -np.cos(place)
    weights = math.pi / NQ1 * np.sin(place)
    values = [np.ones(NQ1), points]
    slopes = [np.zeros(NQ1), np.ones(NQ1)]
    for n in range(1, P1 - 1):
        values.append(((2 * n + 1) * points * values[n] - n * values[n - 1]) / (n + 1))
        slopes.append(slopes[n - 1] + (2 * n + 1) * values[n])
    norm = np.sqrt((2 * np.arange(P1) + 1) / 2.0)
    vt = np.stack(values, axis=1) * norm
    st = np.stack(slopes, axis=1) * norm
    ends = [norm * (-1.0) ** np.arange(P1), norm]
    return vt, st, ends, weights


def split(table):
    high = table.astype(np.float32).astype(ml_dtypes.bfloat16)
    low = (table - high.astype(np.float64)).astype(np.float32).astype(ml_dtypes.bfloat16)
    return high, low


def against_split(table):
    rows, depth = table.shape
    pad = MPAD if depth == MODES else TM
    high, low = split(table)
    out = np.zeros((rows, 3 * pad), ml_dtypes.bfloat16)
    out[:, :depth] = high
    out[:, pad : pad + depth] = high
    out[:, 2 * pad : 2 * pad + depth] = low
    return out


def padded(table, rows):
    return np.concatenate([table, np.zeros((rows - table.shape[0],) + table.shape[1:])])


def tables():
    vt, st, ends, w = line_tables()

    def plane(a, first, second, third):
        return np.einsum("i,bj,ck->bcijk", first[a], second, third).reshape(NQ1 * NQ1, MODES)

    face_w = np.outer(w, w).reshape(-1, 1)
    vol_u, vol_p = [], []
    for a in range(NQ1):
        grads = [plane(a, st, vt, vt), plane(a, vt, st, vt), plane(a, vt, vt, st)]
        vol_u.append(np.concatenate([padded(t, PT) for t in [plane(a, vt, vt, vt)] + grads]))
        vol_p.append(padded(np.concatenate([padded(w[a] * face_w * t, PT) for t in grads]), 176))
    eye = np.eye(P1)

    def face(f, tangent):
        e = ends[f % 2][None]
        parts = [e, tangent, tangent] if f < 2 else [tangent, e, tangent] if f < 4 else [tangent, tangent, e]
        out = np.einsum("ai,bj,ck->abcijk", *parts)
        return out.reshape(-1, MODES)

    modal = [padded(face(f, eye), TM) for f in (1, 0, 3, 2, 5, 4)]
    at_points = [padded(face(f, vt), PT) for f in range(6)]
    weighted = [padded(face_w * face(f, vt), PT) for f in range(6)]
    face_u = np.concatenate(modal + at_points)
    face_p = np.concatenate(weighted)
    tangents = padded(np.einsum("bj,ck->bcjk", vt, vt).reshape(NQ1 * NQ1, P1 * P1), 64)
    return (
        np.stack([against_split(t) for t in vol_u]),
        np.stack([against_split(t) for t in vol_p]),
        against_split(face_u),
        against_split(face_p),
        against_split(tangents),
    )


def dot(a, b):
    return lax.dot_general(a, b, (((1,), (0,)), ((), ())), preferred_element_type=F32)


def dot_rows(a, b):
    return lax.dot_general(a, b, (((1,), (1,)), ((), ())), preferred_element_type=F32)


def halves(x):
    high = x.astype(BF16)
    return high, (x - high.astype(F32)).astype(BF16)


def thirds(x):
    high = x.astype(BF16)
    rest = x - high.astype(F32)
    mid = rest.astype(BF16)
    return high, mid, (rest - mid.astype(F32)).astype(BF16)


def digit_sum(m, step, count):
    total = jnp.zeros(m.shape, jnp.int32)
    for n in range(1, count):
        total = total + jnp.where(m >= n * step, 1, 0)
    return total


def top_of(rows):
    m = lax.broadcasted_iota(jnp.int32, (rows, ELEM), 0)
    i = digit_sum(m, P1 * P1, P1)
    m = m - i * (P1 * P1)
    j = digit_sum(m, P1, P1)
    k = m - j * P1
    return jnp.maximum(jnp.maximum(i, j), k)


def factor_top(rows):
    m = lax.broadcasted_iota(jnp.int32, (rows, ELEM), 0)
    i = digit_sum(m, 3 * P1, P1)
    j = digit_sum(m - i * (3 * P1), 3, P1)
    return jnp.maximum(i, j)


def speed(values, lead):
    return lead * lax.rsqrt(1.0 + values * values)


def work(
    state_hbm,
    adjoint_hbm,
    factors_hbm,
    order_hbm,
    marks_hbm,
    neighbours_hbm,
    owner_hbm,
    vol_u_hbm,
    vol_p_hbm,
    face_u_hbm,
    face_p_hbm,
    tangents_hbm,
    recv,
    share,
    owner,
    order,
    marks,
    state,
    factors,
    adjoint,
    neighbours,
    tangents,
    vol_u,
    vol_p,
    face_u,
    face_p,
    send,
    sel,
    top,
    padded_x,
    fac,
    fac3,
    us,
    ps,
    hsend,
    outer,
    own,
    own_p,
    vals,
    vals_p,
    near,
    gath,
    leaf_sum,
    row_sum,
    grp_sum,
    load_sem,
    self_sem,
    send_sem,
    recv_sem,
    halo_send,
    halo_recv,
    leaf_send,
    leaf_recv,
    row_send,
    row_recv,
    sum_send,
    sum_recv,
):
    g = lax.axis_index("grp")
    r = lax.axis_index("dom")
    lane = lax.rem(r, LEAF)
    row = r // LEAF
    after = lax.rem(r + 1, DOM)
    before = lax.rem(r + DOM - 1, DOM)

    barrier = pltpu.get_barrier_semaphore()

    def greet(to_g, to_r):
        pl.semaphore_signal(barrier, inc=1, device_id=(to_g, to_r), device_id_type=MESH)

    @pl.loop(1, GRP)
    def _(k):
        greet(lax.rem(g + k, GRP), r)

    @pl.loop(1, LEAF)
    def _(k):
        greet(g, row * LEAF + lax.rem(lane + k, LEAF))

    @pl.loop(1, ROWS)
    def _(k):
        greet(g, lax.rem(row + k, ROWS) * LEAF + lane)

    greet(g, after)
    greet(g, before)
    greeted = GRP + LEAF + ROWS - 1

    loads = [
        pltpu.make_async_copy(source, target, load_sem.at[n])
        for n, (source, target) in enumerate(
            (
                (owner_hbm, owner),
                (order_hbm, order),
                (marks_hbm, marks),
                (state_hbm, state),
                (factors_hbm, factors),
                (adjoint_hbm, adjoint),
                (face_u_hbm, face_u),
                (neighbours_hbm, neighbours),
                (tangents_hbm, tangents),
                (vol_u_hbm, vol_u),
                (vol_p_hbm, vol_p),
                (face_p_hbm, face_p),
            )
        )
    ]
    for load in loads:
        load.start()
    for load in loads[:5]:
        load.wait()

    to = owner[...]
    hits = jnp.where(lax.broadcasted_iota(jnp.int32, (GRP, ELEM), 0) == to, 1.0, 0.0)
    earlier = jnp.where(
        lax.broadcasted_iota(jnp.int32, (ELEM, ELEM), 0)
        < lax.broadcasted_iota(jnp.int32, (ELEM, ELEM), 1),
        1.0,
        0.0,
    ).astype(BF16)
    counts = dot(hits.astype(BF16), earlier)
    rank = jnp.sum(hits * counts, axis=0, keepdims=True).astype(jnp.int32)
    slot = to * CAP + rank
    sel[...] = jnp.where(
        lax.broadcasted_iota(jnp.int32, (SLOTS, ELEM), 0) == slot, 1.0, 0.0
    ).astype(BF16)

    level = order[...]
    fresh = jnp.clip(level + marks[...], 1, PMAX)
    low = jnp.minimum(level, fresh)
    top[...] = top_of(MPAD)

    for i in range(P1):
        for j in range(P1):
            at = (i * P1 + j) * 3
            fac[at : at + 3, :] = factors[i, j]
    fac[FROWS - 1 : 80, :] = jnp.zeros((80 - FROWS + 1, ELEM), F32)
    rows = lax.broadcasted_iota(jnp.int32, (80, ELEM), 0)
    kept = jnp.where(factor_top(80) <= low, fac[...], 0.0)
    fac[...] = jnp.where(rows == FROWS - 1, fresh.astype(F32), kept)
    for n in range(2 * NV):
        fac3[n, 0:SPARE, :] = fac[n * SPARE : (n + 1) * SPARE, :]

    def pack(source, v, most, column):
        padded_x[0:MODES, :] = jnp.where(top[0:MODES, :] <= most, source[v], 0.0)
        padded_x[MODES:MPAD, :] = fac3[column, 0:SPARE, :]
        high, mid, tail = thirds(padded_x[...])
        chosen = sel[...]
        out = dot_rows(chosen, tail) + dot_rows(chosen, mid) + dot_rows(chosen, high)
        place = pl.ds(pl.multiple_of(column * CAP, 8), CAP)
        send[:, place, :] = out.reshape(GRP, CAP, MPAD)

    def pack_rest():
        total = jnp.zeros((GRP * 8, MPAD), F32)
        line = lax.broadcasted_iota(jnp.int32, (GRP * 8, ELEM), 0)
        line_slot = (line // 8) * CAP + lax.rem(line, 8)
        from_row = 2 * NV * SPARE - REST_AT
        rest = fac[from_row : from_row + REST + 8, :]
        rest = jnp.concatenate([rest, jnp.zeros((MPAD - REST - 8, ELEM), F32)], axis=0)
        rest = jnp.where(lax.broadcasted_iota(jnp.int32, (MPAD, ELEM), 0) < REST_AT, 0.0, rest)
        for part in range(3):
            chosen = jnp.where(line_slot + 8 * part == slot, 1.0, 0.0).astype(BF16)
            moved = rest if part == 0 else pltpu.roll(rest, REST * part, 0)
            for piece in reversed(thirds(moved)):
                total = total + dot_rows(chosen, piece)
        send[:, COLS * CAP : BLOCK, :] = total.reshape(GRP, 8, MPAD)

    def block_to(ahead, n, first, count):
        to_g = lax.rem(g + ahead + GRP, GRP)
        rows = pl.ds(first, count)
        return pltpu.make_async_remote_copy(
            src_ref=send.at[to_g, rows],
            dst_ref=recv.at[g, rows],
            send_sem=send_sem.at[n],
            recv_sem=recv_sem.at[n],
            device_id=(to_g, r),
            device_id_type=MESH,
        )

    partners = [k for d in range(1, GRP // 2) for k in (d, -d)] + [GRP // 2]
    blocks = {}
    for k in partners:
        n = len(blocks) if not blocks else max(blocks.values(), key=lambda x: x[-1][1])[-1][1] + 1
        if abs(k) <= NEAR:
            cut = [0] + [(c + count) * CAP for c, count in PIECES[:-1]] + [BLOCK]
            blocks[k] = [(p, n + p, cut[p], cut[p + 1] - cut[p]) for p in range(len(PIECES))]
        else:
            blocks[k] = [(0, n, 0, BLOCK)]

    def send_block(k, p=0):
        block_to(k, *blocks[k][p][1:]).start()

    def send_piece(p):
        for k in partners:
            if abs(k) <= NEAR:
                send_block(k, p)

    own_block = pltpu.make_async_copy(send.at[g], recv.at[g], self_sem)

    def pack_columns(first, count):
        @pl.loop(first, min(first + count, NV))
        def _(c):
            pack(state, c, low, c)

        @pl.loop(max(first, NV), first + count)
        def _(c):
            pack(adjoint, c - NV, fresh, c)

    for p, (first, count) in enumerate(PIECES):
        if first <= NV < first + count or first == NV:
            loads[5].wait()
        pack_columns(first, count)
        if p == 0:
            pl.semaphore_wait(barrier, greeted)
        if p == len(PIECES) - 1:
            pack_rest()
        send_piece(p)
    for k in partners:
        if NEAR < abs(k) <= BEFORE:
            send_block(k)
    own_block.start()

    def split_into(target, source, v, most):
        padded_x[0:MODES, :] = jnp.where(top[0:MODES, :] <= most, source[v], 0.0)
        padded_x[MODES:MPAD, :] = jnp.zeros((SPARE, ELEM), F32)
        high, tail = halves(padded_x[...])
        target[v, 0:MPAD, :] = high
        target[v, MPAD : 2 * MPAD, :] = tail
        target[v, 2 * MPAD :, :] = high

    loads[6].wait()

    @pl.loop(0, NV)
    def _(v):
        split_into(us, state, v, level)
        both = dot(face_u[...], us[v])
        place = pl.ds(pl.multiple_of(v * TM, TM), TM)
        for b in range(4):
            outer[b, place, :] = both[b * TM : (b + 1) * TM]
        hsend[0, place, :] = both[4 * TM : 5 * TM]
        hsend[1, place, :] = both[5 * TM : 6 * TM]
        for f in range(6):
            own[f, v] = both[6 * TM + f * PT : 6 * TM + (f + 1) * PT]

    halos = [
        pltpu.make_async_remote_copy(
            src_ref=hsend.at[n],
            dst_ref=outer.at[4 + n],
            send_sem=halo_send.at[n],
            recv_sem=halo_recv.at[n],
            device_id=(g, to_r),
            device_id_type=MESH,
        )
        for n, to_r in enumerate((after, before))
    ]
    for halo in halos:
        halo.start()

    @pl.loop(0, NV)
    def _(v):
        split_into(ps, adjoint, v, level + 1)

    loads[9].wait()
    loads[10].wait()
    near[...] = jnp.zeros(near.shape, F32)

    @pl.loop(0, NQ1)
    def _(a):
        @pl.loop(0, NV)
        def _(v):
            vals[v] = dot(vol_u[a], us[v])
            vals_p[v] = dot(vol_p[a], ps[v])

        @pl.loop(0, PT // 8)
        def _(t):
            def at(table, v):
                return vals[v, pl.ds(pl.multiple_of(table * PT + t * 8, 8), 8), :]

            def at_p(table, v):
                return vals_p[v, pl.ds(pl.multiple_of(table * PT + t * 8, 8), 8), :]

            u0 = at(0, 0)
            inverse = lax.rsqrt(1.0 + u0 * u0)
            c = [at(0, 1 + d) * inverse for d in range(3)]
            u5 = at(0, 5)
            soft = jnp.maximum(u5, 0.0) + jnp.log1p(jnp.exp(-jnp.abs(u5)))
            nu = 0.05 + 0.1 * soft
            total = jnp.zeros((8, ELEM), F32)
            for v in range(NV):
                w = [at_p(d, v) for d in range(3)]
                carried = w[0] * c[0] + w[1] * c[1] + w[2] * c[2]
                spread = w[0] * at(1, v) + w[1] * at(2, v) + w[2] * at(3, v)
                total = total + (carried * at(0, v) - nu * spread)
            near[...] = near[...] - total

    loads[11].wait()
    loads[7].wait()
    loads[8].wait()

    @pl.loop(0, NV)
    def _(v):
        both = dot(face_p[...], ps[v])
        for f in range(6):
            own_p[f, v] = both[f * PT : (f + 1) * PT]

    for halo in halos:
        halo.wait()

    @pl.loop(0, 6)
    def _(f):
        absent = jnp.where(f == 4, jnp.where(r == 0, 1, 0), 0) + jnp.where(
            f == 5, jnp.where(r == DOM - 1, 1, 0), 0
        )
        present = 1.0 - absent.astype(F32)
        high, tail = halves(outer[f] * present)
        source = lax.broadcasted_iota(jnp.int32, (ELEM, ELEM), 0)
        pick = jnp.where(source == neighbours[pl.ds(f, 1), :], 1.0, 0.0).astype(BF16)
        got_high = dot(high, pick).astype(BF16)
        got_tail = dot(tail, pick).astype(BF16)
        for v in range(NV):
            lanes = slice(v * ELEM, (v + 1) * ELEM)
            gath[0:TM, lanes] = got_high[v * TM : (v + 1) * TM]
            gath[TM : 2 * TM, lanes] = got_tail[v * TM : (v + 1) * TM]
            gath[2 * TM :, lanes] = got_high[v * TM : (v + 1) * TM]
        seen = dot(tangents[...], gath[...])
        o = [seen[0:PT, v * ELEM : (v + 1) * ELEM] for v in range(NV)]
        d = f // 2
        sign = (2 * lax.rem(f, 2) - 1).astype(F32)
        lead_o = jnp.where(d == 0, o[1], jnp.where(d == 1, o[2], o[3]))
        half = 0.5 * sign
        speed_t = half * speed(own[f, 0], own[f, 1 + d])
        speed_o = half * speed(o[0], lead_o)
        total = jnp.zeros((PT, ELEM), F32)
        for v in range(NV):
            t = own[f, v]
            total = total + own_p[f, v] * (
                speed_t * t + speed_o * o[v] + 0.5 * (t - o[v])
            )
        part = total[0:8]
        for n in range(1, PT // 8):
            part = part + total[n * 8 : (n + 1) * 8]
        near[...] = near[...] + part

    eta = jnp.abs(jnp.sum(near[...], axis=0, keepdims=True))

    def exchange(buffer, mine, count, send_s, recv_s, device, then):
        def one(k):
            return pltpu.make_async_remote_copy(
                src_ref=buffer.at[mine],
                dst_ref=buffer.at[mine],
                send_sem=send_s.at[k],
                recv_sem=recv_s.at[k],
                device_id=device(k),
                device_id_type=MESH,
            )

        @pl.loop(1, count)
        def _(k):
            one(k).start()

        for k in partners:
            if abs(k) in then:
                send_block(k)

        @pl.loop(1, count)
        def _(k):
            one(k).wait()

        return jnp.sum(buffer[...], axis=0)

    leaf_sum[lane] = jnp.broadcast_to(jnp.sum(eta, axis=1, keepdims=True), (8, 128))
    part = exchange(
        leaf_sum, lane, LEAF, leaf_send, leaf_recv,
        lambda k: (g, row * LEAF + lax.rem(lane + k, LEAF)),
        (BEFORE + 1,),
    )
    row_sum[row] = part
    part = exchange(
        row_sum, row, ROWS, row_send, row_recv,
        lambda k: (g, lax.rem(row + k, ROWS) * LEAF + lane),
        (BEFORE + 2,),
    )
    grp_sum[g] = part
    part = exchange(
        grp_sum, g, GRP, sum_send, sum_recv, lambda k: (lax.rem(g + k, GRP), r),
        range(BEFORE + 3, GRP),
    )
    mean = part[0:1, 0:1] / (ELEM * GRP * DOM)
    share[...] = eta / (mean + 1e-06)

    own_block.wait()
    for k in partners:
        for piece in blocks[k]:
            block_to(k, *piece[1:]).wait()


def unpack(
    recv,
    share_in,
    moved_state,
    moved_adjoint,
    moved_factors,
    moved_order,
    share,
    columns,
    spare,
    factors,
    order,
    sem,
):
    copies = []

    def put(source, target):
        copy = pltpu.make_async_copy(source, target, sem.at[len(copies)])
        copy.start()
        copies.append(copy)

    put(share_in, share)
    for c in range(COLS):
        lines = recv[:, c * CAP : (c + 1) * CAP, :].reshape(SLOTS, MPAD).T
        columns[c] = lines[0:MODES]
        spare[c, 0:SPARE, :] = lines[MODES:MPAD]
        target = moved_state.at[c] if c < NV else moved_adjoint.at[c - NV]
        put(columns.at[c], target)
    rest = recv[:, COLS * CAP : BLOCK, :].reshape(GRP * 8, MPAD)
    parts = [rest] + [pltpu.roll(rest, MPAD - REST * n, 1) for n in (1, 2)]
    parts = [part.reshape(GRP, 1, 8, MPAD) for part in parts]
    lines = jnp.concatenate(parts, axis=1).reshape(SLOTS, MPAD).T
    rows = [spare[c, 0:SPARE, :] for c in range(COLS)]
    whole = jnp.concatenate(rows + [lines[REST_AT : REST_AT + REST]], axis=0)
    for i in range(P1):
        for j in range(P1):
            at = (i * P1 + j) * 3
            factors[i, j] = whole[at : at + 3]
    put(factors, moved_factors)
    order[...] = whole[FROWS - 1 : FROWS].astype(jnp.int32)
    put(order, moved_order)
    for copy in copies:
        copy.wait()


def body(state, adjoint, factors, order, marks, neighbours, new_owner):
    vol_u, vol_p, face_u, face_p, tangents = [jnp.asarray(t) for t in tables()]
    hbm = pl.BlockSpec(memory_space=pltpu.HBM)
    vmem = pl.BlockSpec(memory_space=pltpu.VMEM)
    dma = pltpu.SemaphoreType.DMA
    copies = GRP - 1 + 2 * NEAR * (len(PIECES) - 1)
    arrays = (
        state,
        adjoint,
        factors.transpose(1, 2, 0, 3),
        order.reshape(1, ELEM),
        marks.reshape(1, ELEM),
        neighbours,
        new_owner.reshape(1, ELEM),
        vol_u,
        vol_p,
        face_u,
        face_p,
        tangents,
    )
    recv, share = pl.pallas_call(
        work,
        name="indicator_and_send",
        out_shape=(
            pltpu.VMEM((GRP, BLOCK, MPAD), F32),
            pltpu.VMEM((1, ELEM), F32),
        ),
        in_specs=[hbm] * len(arrays),
        out_specs=(vmem, vmem),
        scratch_shapes=[
            pltpu.VMEM((1, ELEM), jnp.int32),
            pltpu.VMEM((1, ELEM), jnp.int32),
            pltpu.VMEM((1, ELEM), jnp.int32),
            pltpu.VMEM((NV, MODES, ELEM), F32),
            pltpu.VMEM((P1, P1, 3, ELEM), F32),
            pltpu.VMEM((NV, MODES, ELEM), F32),
            pltpu.VMEM((6, ELEM), jnp.int32),
            pltpu.VMEM(tangents.shape, BF16),
            pltpu.VMEM(vol_u.shape, BF16),
            pltpu.VMEM(vol_p.shape, BF16),
            pltpu.VMEM(face_u.shape, BF16),
            pltpu.VMEM(face_p.shape, BF16),
            pltpu.VMEM((GRP, BLOCK, MPAD), F32),
            pltpu.VMEM((SLOTS, ELEM), BF16),
            pltpu.VMEM((MPAD, ELEM), jnp.int32),
            pltpu.VMEM((MPAD, ELEM), F32),
            pltpu.VMEM((80, ELEM), F32),
            pltpu.VMEM((2 * NV, 8, ELEM), F32),
            pltpu.VMEM((NV, KCAT, ELEM), BF16),
            pltpu.VMEM((NV, KCAT, ELEM), BF16),
            pltpu.VMEM((2, NV * TM, ELEM), F32),
            pltpu.VMEM((6, NV * TM, ELEM), F32),
            pltpu.VMEM((6, NV, PT, ELEM), F32),
            pltpu.VMEM((6, NV, PT, ELEM), F32),
            pltpu.VMEM((NV, 4 * PT, ELEM), F32),
            pltpu.VMEM((NV, 176, ELEM), F32),
            pltpu.VMEM((8, ELEM), F32),
            pltpu.VMEM((3 * TM, NV * ELEM), BF16),
            pltpu.VMEM((LEAF, 8, 128), F32),
            pltpu.VMEM((ROWS, 8, 128), F32),
            pltpu.VMEM((GRP, 8, 128), F32),
            dma((12,)),
            dma,
            dma((copies,)),
            dma((copies,)),
            dma((2,)),
            dma((2,)),
            dma((LEAF,)),
            dma((LEAF,)),
            dma((ROWS,)),
            dma((ROWS,)),
            dma((GRP,)),
            dma((GRP,)),
        ],
        compiler_params=pltpu.CompilerParams(
            collective_id=0, has_side_effects=True, vmem_limit_bytes=32 << 20
        ),
    )(*[pltpu.with_memory_space_constraint(x, pltpu.HBM) for x in arrays])
    moved_state, moved_adjoint, moved_factors, moved_order, share = pl.pallas_call(
        unpack,
        name="unpack_slots",
        out_shape=(
            jax.ShapeDtypeStruct((NV, MODES, SLOTS), F32),
            jax.ShapeDtypeStruct((NV, MODES, SLOTS), F32),
            jax.ShapeDtypeStruct((P1, P1, 3, SLOTS), F32),
            jax.ShapeDtypeStruct((1, SLOTS), jnp.int32),
            jax.ShapeDtypeStruct((1, ELEM), F32),
        ),
        in_specs=[vmem, vmem],
        out_specs=(hbm,) * 5,
        scratch_shapes=[
            pltpu.VMEM((COLS, MODES, SLOTS), F32),
            pltpu.VMEM((COLS, 8, SLOTS), F32),
            pltpu.VMEM((P1, P1, 3, SLOTS), F32),
            pltpu.VMEM((1, SLOTS), jnp.int32),
            dma((COLS + 3,)),
        ],
        compiler_params=pltpu.CompilerParams(vmem_limit_bytes=24 << 20),
    )(*[pltpu.with_memory_space_constraint(x, pltpu.VMEM) for x in (recv, share)])
    return (
        share.reshape(ELEM),
        moved_state,
        moved_adjoint,
        moved_factors.transpose(2, 0, 1, 3),
        moved_order.reshape(SLOTS),
    )


def solution(mesh):
    return jax.shard_map(
        body,
        mesh=mesh,
        in_specs=(
            P(None, None, ("grp", "dom")),
            P(None, None, ("grp", "dom")),
            P(None, None, None, ("grp", "dom")),
            P(("grp", "dom")),
            P(("grp", "dom")),
            P(None, ("grp", "dom")),
            P(("grp", "dom"), None),
        ),
        out_specs=(
            P(("grp", "dom")),
            P(None, None, ("grp", "dom")),
            P(None, None, ("grp", "dom")),
            P(None, None, None, ("grp", "dom")),
            P(("grp", "dom")),
        ),
        check_vma=False,
    )
```

```python
import functools
import math

import jax
import jax.numpy as jnp
import ml_dtypes
import numpy as np
from jax import lax
from jax.experimental import pallas as pl
from jax.experimental.pallas import tpu as pltpu
from jax.sharding import PartitionSpec as P

NV = 6
PMAX = 4
P1 = 5
MODES = 125
NQ1 = 7
ELEM = 256
CAP = 24
GRP = 16
DOM = 32
SLOTS = GRP * CAP
LEAF = 8
ROWS = DOM // LEAF
MPAD = 128
PT = 56
TM = 32
KCAT = 3 * MPAD
FROWS = 3 * P1 * P1 + 1
SPARE = MPAD - MODES
REST = FROWS - 2 * NV * SPARE
REST_AT = 2 * NV * SPARE % 8
MESH = pl.DeviceIdType.MESH
COLS = 2 * NV
BLOCK = COLS * CAP + 8
PIECES = ((0, 1), (1, 2), (3, 3), (6, 3), (9, 3))
NEAR = 2
FIRST = (3, 8)
LATER = ((7,), (6,), (5, 4))
F32 = jnp.float32
BF16 = jnp.bfloat16


def line_tables():
    place = math.pi * (np.arange(NQ1) + 0.5) / NQ1
    points = -np.cos(place)
    weights = math.pi / NQ1 * np.sin(place)
    values = [np.ones(NQ1), points]
    slopes = [np.zeros(NQ1), np.ones(NQ1)]
    for n in range(1, P1 - 1):
        values.append(((2 * n + 1) * points * values[n] - n * values[n - 1]) / (n + 1))
        slopes.append(slopes[n - 1] + (2 * n + 1) * values[n])
    norm = np.sqrt((2 * np.arange(P1) + 1) / 2.0)
    vt = np.stack(values, axis=1) * norm
    st = np.stack(slopes, axis=1) * norm
    ends = [norm * (-1.0) ** np.arange(P1), norm]
    return vt, st, ends, weights


def split(table):
    high = table.astype(np.float32).astype(ml_dtypes.bfloat16)
    low = (table - high.astype(np.float64)).astype(np.float32).astype(ml_dtypes.bfloat16)
    return high, low


def against_split(table):
    rows, depth = table.shape
    pad = MPAD if depth == MODES else TM
    high, low = split(table)
    out = np.zeros((rows, 3 * pad), ml_dtypes.bfloat16)
    out[:, :depth] = high
    out[:, pad : pad + depth] = high
    out[:, 2 * pad : 2 * pad + depth] = low
    return out


def padded(table, rows):
    return np.concatenate([table, np.zeros((rows - table.shape[0],) + table.shape[1:])])


def tables():
    vt, st, ends, w = line_tables()

    def plane(a, first, second, third):
        return np.einsum("i,bj,ck->bcijk", first[a], second, third).reshape(NQ1 * NQ1, MODES)

    face_w = np.outer(w, w).reshape(-1, 1)
    vol_u, vol_p = [], []
    for a in range(NQ1):
        grads = [plane(a, st, vt, vt), plane(a, vt, st, vt), plane(a, vt, vt, st)]
        vol_u.append(np.concatenate([padded(t, PT) for t in [plane(a, vt, vt, vt)] + grads]))
        vol_p.append(padded(np.concatenate([padded(w[a] * face_w * t, PT) for t in grads]), 176))
    eye = np.eye(P1)

    def face(f, tangent):
        e = ends[f % 2][None]
        parts = [e, tangent, tangent] if f < 2 else [tangent, e, tangent] if f < 4 else [tangent, tangent, e]
        out = np.einsum("ai,bj,ck->abcijk", *parts)
        return out.reshape(-1, MODES)

    modal = [padded(face(f, eye), TM) for f in (1, 0, 3, 2, 5, 4)]
    at_points = [padded(face(f, vt), PT) for f in range(6)]
    weighted = [padded(face_w * face(f, vt), PT) for f in range(6)]
    face_u = np.concatenate(modal + at_points)
    face_p = np.concatenate(weighted)
    tangents = padded(np.einsum("bj,ck->bcjk", vt, vt).reshape(NQ1 * NQ1, P1 * P1), 64)
    return (
        np.stack([against_split(t) for t in vol_u]),
        np.stack([against_split(t) for t in vol_p]),
        against_split(face_u),
        against_split(face_p),
        against_split(tangents),
    )


def dot(a, b):
    return lax.dot_general(a, b, (((1,), (0,)), ((), ())), preferred_element_type=F32)


def dot_rows(a, b):
    return lax.dot_general(a, b, (((1,), (1,)), ((), ())), preferred_element_type=F32)


def halves(x):
    high = x.astype(BF16)
    return high, (x - high.astype(F32)).astype(BF16)


def thirds(x):
    high = x.astype(BF16)
    rest = x - high.astype(F32)
    mid = rest.astype(BF16)
    return high, mid, (rest - mid.astype(F32)).astype(BF16)


def digit_sum(m, step, count):
    total = jnp.zeros(m.shape, jnp.int32)
    for n in range(1, count):
        total = total + jnp.where(m >= n * step, 1, 0)
    return total


def top_of(rows):
    m = lax.broadcasted_iota(jnp.int32, (rows, ELEM), 0)
    i = digit_sum(m, P1 * P1, P1)
    m = m - i * (P1 * P1)
    j = digit_sum(m, P1, P1)
    k = m - j * P1
    return jnp.maximum(jnp.maximum(i, j), k)


def factor_top(rows):
    m = lax.broadcasted_iota(jnp.int32, (rows, ELEM), 0)
    i = digit_sum(m, 3 * P1, P1)
    j = digit_sum(m - i * (3 * P1), 3, P1)
    return jnp.maximum(i, j)


def speed(values, lead):
    return lead * lax.rsqrt(1.0 + values * values)


def work(
    state_hbm,
    adjoint_hbm,
    factors_hbm,
    order_hbm,
    marks_hbm,
    neighbours_hbm,
    owner_hbm,
    vol_u_hbm,
    vol_p_hbm,
    face_u_hbm,
    face_p_hbm,
    tangents_hbm,
    recv,
    share,
    owner,
    order,
    marks,
    state,
    factors,
    adjoint,
    neighbours,
    tangents,
    vol_u,
    vol_p,
    face_u,
    face_p,
    send,
    sel,
    top,
    padded_x,
    fac,
    fac3,
    us,
    ps,
    hsend,
    outer,
    own,
    own_p,
    vals,
    vals_p,
    near,
    gath,
    leaf_sum,
    row_sum,
    grp_sum,
    load_sem,
    self_sem,
    send_sem,
    recv_sem,
    halo_send,
    halo_recv,
    leaf_send,
    leaf_recv,
    row_send,
    row_recv,
    sum_send,
    sum_recv,
    grp_in,
    dom_in,
):
    g = lax.axis_index("grp")
    r = lax.axis_index("dom")
    lane = lax.rem(r, LEAF)
    row = r // LEAF
    after = lax.rem(r + 1, DOM)
    before = lax.rem(r + DOM - 1, DOM)

    barrier = pltpu.get_barrier_semaphore()

    def greet(to_g, to_r):
        pl.semaphore_signal(barrier, inc=1, device_id=(to_g, to_r), device_id_type=MESH)

    greet(lax.rem(g + 1, GRP), r)
    greet(lax.rem(g + GRP - 1, GRP), r)
    greet(g, after)
    greet(g, before)
    greeted = 4

    def tell_grp(n):
        for to_g in (lax.rem(g + 2**n, GRP), lax.rem(g + GRP - 2**n, GRP)):
            pl.semaphore_signal(
                grp_in.at[n], inc=1, device_id=(to_g, r), device_id_type=MESH
            )

    def tell_dom(n):
        for to_r in (lax.rem(r + 2**n, DOM), lax.rem(r + DOM - 2**n, DOM)):
            pl.semaphore_signal(
                dom_in.at[n], inc=1, device_id=(g, to_r), device_id_type=MESH
            )

    def told_dom(n):
        pl.semaphore_wait(dom_in.at[n], 2)
        if n < 3:
            tell_dom(n + 1)

    def told_grp(n):
        pl.semaphore_wait(grp_in.at[n], 2)
        if n < 2:
            tell_grp(n + 1)

    loads = [
        pltpu.make_async_copy(source, target, load_sem.at[n])
        for n, (source, target) in enumerate(
            (
                (owner_hbm, owner),
                (order_hbm, order),
                (marks_hbm, marks),
                (factors_hbm, factors),
                (state_hbm, state),
                (adjoint_hbm, adjoint),
                (face_u_hbm, face_u),
                (neighbours_hbm, neighbours),
                (tangents_hbm, tangents),
                (vol_u_hbm, vol_u),
                (vol_p_hbm, vol_p),
                (face_p_hbm, face_p),
            )
        )
    ]
    for load in loads:
        load.start()

    top[...] = top_of(MPAD)
    loads[0].wait()
    to = owner[...]
    hits = jnp.where(lax.broadcasted_iota(jnp.int32, (GRP, ELEM), 0) == to, 1.0, 0.0)
    earlier = jnp.where(
        lax.broadcasted_iota(jnp.int32, (ELEM, ELEM), 0)
        < lax.broadcasted_iota(jnp.int32, (ELEM, ELEM), 1),
        1.0,
        0.0,
    ).astype(BF16)
    counts = dot(hits.astype(BF16), earlier)
    rank = jnp.sum(hits * counts, axis=0, keepdims=True).astype(jnp.int32)
    slot = to * CAP + rank
    sel[...] = jnp.where(
        lax.broadcasted_iota(jnp.int32, (SLOTS, ELEM), 0) == slot, 1.0, 0.0
    ).astype(BF16)

    for load in loads[1:4]:
        load.wait()
    level = order[...]
    fresh = jnp.clip(level + marks[...], 1, PMAX)
    low = jnp.minimum(level, fresh)

    for i in range(P1):
        for j in range(P1):
            at = (i * P1 + j) * 3
            fac[at : at + 3, :] = factors[i, j]
    fac[FROWS - 1 : 80, :] = jnp.zeros((80 - FROWS + 1, ELEM), F32)
    rows = lax.broadcasted_iota(jnp.int32, (80, ELEM), 0)
    kept = jnp.where(factor_top(80) <= low, fac[...], 0.0)
    fac[...] = jnp.where(rows == FROWS - 1, fresh.astype(F32), kept)
    for n in range(2 * NV):
        fac3[n, 0:SPARE, :] = fac[n * SPARE : (n + 1) * SPARE, :]

    def pack(source, v, most, column):
        padded_x[0:MODES, :] = jnp.where(top[0:MODES, :] <= most, source[v], 0.0)
        padded_x[MODES:MPAD, :] = fac3[column, 0:SPARE, :]
        high, mid, tail = thirds(padded_x[...])
        chosen = sel[...]
        out = dot_rows(chosen, tail) + dot_rows(chosen, mid) + dot_rows(chosen, high)
        place = pl.ds(pl.multiple_of(column * CAP, 8), CAP)
        send[:, place, :] = out.reshape(GRP, CAP, MPAD)

    def pack_rest():
        total = jnp.zeros((GRP * 8, MPAD), F32)
        line = lax.broadcasted_iota(jnp.int32, (GRP * 8, ELEM), 0)
        line_slot = (line // 8) * CAP + lax.rem(line, 8)
        from_row = 2 * NV * SPARE - REST_AT
        rest = fac[from_row : from_row + REST + 8, :]
        rest = jnp.concatenate([rest, jnp.zeros((MPAD - REST - 8, ELEM), F32)], axis=0)
        rest = jnp.where(lax.broadcasted_iota(jnp.int32, (MPAD, ELEM), 0) < REST_AT, 0.0, rest)
        for part in range(3):
            chosen = jnp.where(line_slot + 8 * part == slot, 1.0, 0.0).astype(BF16)
            moved = rest if part == 0 else pltpu.roll(rest, REST * part, 0)
            for piece in reversed(thirds(moved)):
                total = total + dot_rows(chosen, piece)
        send[:, COLS * CAP : BLOCK, :] = total.reshape(GRP, 8, MPAD)

    def block_to(ahead, n, first, count):
        to_g = lax.rem(g + ahead + GRP, GRP)
        rows = pl.ds(first, count)
        return pltpu.make_async_remote_copy(
            src_ref=send.at[to_g, rows],
            dst_ref=recv.at[g, rows],
            send_sem=send_sem.at[n],
            recv_sem=recv_sem.at[n],
            device_id=(to_g, r),
            device_id_type=MESH,
        )

    partners = [k for d in range(1, GRP // 2) for k in (d, -d)] + [GRP // 2]
    blocks = {}
    for k in partners:
        n = len(blocks) if not blocks else max(blocks.values(), key=lambda x: x[-1][1])[-1][1] + 1
        if abs(k) <= NEAR:
            cut = [0] + [(c + count) * CAP for c, count in PIECES[:-1]] + [BLOCK]
            blocks[k] = [(p, n + p, cut[p], cut[p + 1] - cut[p]) for p in range(len(PIECES))]
        else:
            blocks[k] = [(0, n, 0, BLOCK)]

    def send_block(k, p=0):
        block_to(k, *blocks[k][p][1:]).start()

    def send_piece(p, distance):
        send_block(distance, p)
        send_block(-distance, p)

    own_block = pltpu.make_async_copy(send.at[g], recv.at[g], self_sem)

    def pack_columns(first, count):
        @pl.loop(first, min(first + count, NV))
        def _(c):
            pack(state, c, low, c)

        @pl.loop(max(first, NV), first + count)
        def _(c):
            pack(adjoint, c - NV, fresh, c)

    loads[4].wait()
    for p, (first, count) in enumerate(PIECES):
        if first <= NV < first + count or first == NV:
            loads[5].wait()
        pack_columns(first, count)
        if p == 0:
            pl.semaphore_wait(barrier, greeted)
            tell_grp(0)
            tell_dom(0)
        if p == len(PIECES) - 1:
            pack_rest()
        send_piece(p, 1)
        if p == 0:
            told_grp(0)
        send_piece(p, 2)
    told_grp(1)

    def send_far(distances):
        for d in distances:
            send_block(d)
            if 2 * d != GRP:
                send_block(-d)

    send_far(FIRST[:1])
    told_grp(2)
    send_far(FIRST[1:])
    own_block.start()
    told_dom(0)

    def split_into(target, source, v, most):
        padded_x[0:MODES, :] = jnp.where(top[0:MODES, :] <= most, source[v], 0.0)
        padded_x[MODES:MPAD, :] = jnp.zeros((SPARE, ELEM), F32)
        high, tail = halves(padded_x[...])
        target[v, 0:MPAD, :] = high
        target[v, MPAD : 2 * MPAD, :] = tail
        target[v, 2 * MPAD :, :] = high

    loads[6].wait()

    @pl.loop(0, NV)
    def _(v):
        split_into(us, state, v, level)
        both = dot(face_u[...], us[v])
        place = pl.ds(pl.multiple_of(v * TM, TM), TM)
        for b in range(4):
            outer[b, place, :] = both[b * TM : (b + 1) * TM]
        hsend[0, place, :] = both[4 * TM : 5 * TM]
        hsend[1, place, :] = both[5 * TM : 6 * TM]
        for f in range(6):
            own[f, v] = both[6 * TM + f * PT : 6 * TM + (f + 1) * PT]

    halos = [
        pltpu.make_async_remote_copy(
            src_ref=hsend.at[n],
            dst_ref=outer.at[4 + n],
            send_sem=halo_send.at[n],
            recv_sem=halo_recv.at[n],
            device_id=(g, to_r),
            device_id_type=MESH,
        )
        for n, to_r in enumerate((after, before))
    ]
    for halo in halos:
        halo.start()
    told_dom(1)

    @pl.loop(0, NV)
    def _(v):
        split_into(ps, adjoint, v, level + 1)

    told_dom(2)
    loads[9].wait()
    loads[10].wait()
    near[...] = jnp.zeros(near.shape, F32)

    @pl.loop(0, NQ1)
    def _(a):
        @pl.loop(0, NV)
        def _(v):
            vals[v] = dot(vol_u[a], us[v])
            vals_p[v] = dot(vol_p[a], ps[v])

        @pl.loop(0, PT // 8)
        def _(t):
            def at(table, v):
                return vals[v, pl.ds(pl.multiple_of(table * PT + t * 8, 8), 8), :]

            def at_p(table, v):
                return vals_p[v, pl.ds(pl.multiple_of(table * PT + t * 8, 8), 8), :]

            u0 = at(0, 0)
            inverse = lax.rsqrt(1.0 + u0 * u0)
            c = [at(0, 1 + d) * inverse for d in range(3)]
            u5 = at(0, 5)
            soft = jnp.maximum(u5, 0.0) + jnp.log1p(jnp.exp(-jnp.abs(u5)))
            nu = 0.05 + 0.1 * soft
            total = jnp.zeros((8, ELEM), F32)
            for v in range(NV):
                w = [at_p(d, v) for d in range(3)]
                carried = w[0] * c[0] + w[1] * c[1] + w[2] * c[2]
                spread = w[0] * at(1, v) + w[1] * at(2, v) + w[2] * at(3, v)
                total = total + (carried * at(0, v) - nu * spread)
            near[...] = near[...] - total

    loads[11].wait()
    loads[7].wait()
    loads[8].wait()

    @pl.loop(0, NV)
    def _(v):
        both = dot(face_p[...], ps[v])
        for f in range(6):
            own_p[f, v] = both[f * PT : (f + 1) * PT]

    for halo in halos:
        halo.wait()
    told_dom(3)

    @pl.loop(0, 6)
    def _(f):
        absent = jnp.where(f == 4, jnp.where(r == 0, 1, 0), 0) + jnp.where(
            f == 5, jnp.where(r == DOM - 1, 1, 0), 0
        )
        present = 1.0 - absent.astype(F32)
        high, tail = halves(outer[f] * present)
        source = lax.broadcasted_iota(jnp.int32, (ELEM, ELEM), 0)
        pick = jnp.where(source == neighbours[pl.ds(f, 1), :], 1.0, 0.0).astype(BF16)
        got_high = dot(high, pick).astype(BF16)
        got_tail = dot(tail, pick).astype(BF16)
        for v in range(NV):
            lanes = slice(v * ELEM, (v + 1) * ELEM)
            gath[0:TM, lanes] = got_high[v * TM : (v + 1) * TM]
            gath[TM : 2 * TM, lanes] = got_tail[v * TM : (v + 1) * TM]
            gath[2 * TM :, lanes] = got_high[v * TM : (v + 1) * TM]
        seen = dot(tangents[...], gath[...])
        o = [seen[0:PT, v * ELEM : (v + 1) * ELEM] for v in range(NV)]
        d = f // 2
        sign = (2 * lax.rem(f, 2) - 1).astype(F32)
        lead_o = jnp.where(d == 0, o[1], jnp.where(d == 1, o[2], o[3]))
        half = 0.5 * sign
        speed_t = half * speed(own[f, 0], own[f, 1 + d])
        speed_o = half * speed(o[0], lead_o)
        total = jnp.zeros((PT, ELEM), F32)
        for v in range(NV):
            t = own[f, v]
            total = total + own_p[f, v] * (
                speed_t * t + speed_o * o[v] + 0.5 * (t - o[v])
            )
        part = total[0:8]
        for n in range(1, PT // 8):
            part = part + total[n * 8 : (n + 1) * 8]
        near[...] = near[...] + part

    eta = jnp.abs(jnp.sum(near[...], axis=0, keepdims=True))

    def exchange(buffer, mine, count, send_s, recv_s, device, then):
        def one(k):
            return pltpu.make_async_remote_copy(
                src_ref=buffer.at[mine],
                dst_ref=buffer.at[mine],
                send_sem=send_s.at[k],
                recv_sem=recv_s.at[k],
                device_id=device(k),
                device_id_type=MESH,
            )

        @pl.loop(1, count)
        def _(k):
            one(k).start()

        send_far(then)

        @pl.loop(1, count)
        def _(k):
            one(k).wait()

        return jnp.sum(buffer[...], axis=0)

    leaf_sum[lane] = jnp.broadcast_to(jnp.sum(eta, axis=1, keepdims=True), (8, 128))
    part = exchange(
        leaf_sum, lane, LEAF, leaf_send, leaf_recv,
        lambda k: (g, row * LEAF + lax.rem(lane + k, LEAF)),
        LATER[0],
    )
    row_sum[row] = part
    part = exchange(
        row_sum, row, ROWS, row_send, row_recv,
        lambda k: (g, lax.rem(row + k, ROWS) * LEAF + lane),
        LATER[1],
    )
    grp_sum[g] = part
    part = exchange(
        grp_sum, g, GRP, sum_send, sum_recv, lambda k: (lax.rem(g + k, GRP), r),
        LATER[2],
    )
    mean = part[0:1, 0:1] / (ELEM * GRP * DOM)
    share[...] = eta / (mean + 1e-06)

    own_block.wait()
    for k in partners:
        for piece in blocks[k]:
            block_to(k, *piece[1:]).wait()


def unpack(
    recv,
    share_in,
    moved_state,
    moved_adjoint,
    moved_factors,
    moved_order,
    share,
    columns,
    spare,
    factors,
    order,
    sem,
):
    copies = []

    def put(source, target):
        copy = pltpu.make_async_copy(source, target, sem.at[len(copies)])
        copy.start()
        copies.append(copy)

    put(share_in, share)
    for c in range(COLS):
        lines = recv[:, c * CAP : (c + 1) * CAP, :].reshape(SLOTS, MPAD).T
        columns[c] = lines[0:MODES]
        spare[c, 0:SPARE, :] = lines[MODES:MPAD]
        target = moved_state.at[c] if c < NV else moved_adjoint.at[c - NV]
        put(columns.at[c], target)
    rest = recv[:, COLS * CAP : BLOCK, :].reshape(GRP * 8, MPAD)
    parts = [rest] + [pltpu.roll(rest, MPAD - REST * n, 1) for n in (1, 2)]
    parts = [part.reshape(GRP, 1, 8, MPAD) for part in parts]
    lines = jnp.concatenate(parts, axis=1).reshape(SLOTS, MPAD).T
    rows = [spare[c, 0:SPARE, :] for c in range(COLS)]
    whole = jnp.concatenate(rows + [lines[REST_AT : REST_AT + REST]], axis=0)
    for i in range(P1):
        for j in range(P1):
            at = (i * P1 + j) * 3
            factors[i, j] = whole[at : at + 3]
    put(factors, moved_factors)
    order[...] = whole[FROWS - 1 : FROWS].astype(jnp.int32)
    put(order, moved_order)
    for copy in copies:
        copy.wait()


def body(state, adjoint, factors, order, marks, neighbours, new_owner):
    vol_u, vol_p, face_u, face_p, tangents = [jnp.asarray(t) for t in tables()]
    hbm = pl.BlockSpec(memory_space=pltpu.HBM)
    vmem = pl.BlockSpec(memory_space=pltpu.VMEM)
    dma = pltpu.SemaphoreType.DMA
    copies = GRP - 1 + 2 * NEAR * (len(PIECES) - 1)
    arrays = (
        state,
        adjoint,
        factors.transpose(1, 2, 0, 3),
        order.reshape(1, ELEM),
        marks.reshape(1, ELEM),
        neighbours,
        new_owner.reshape(1, ELEM),
        vol_u,
        vol_p,
        face_u,
        face_p,
        tangents,
    )
    recv, share = pl.pallas_call(
        work,
        name="indicator_and_send",
        out_shape=(
            pltpu.VMEM((GRP, BLOCK, MPAD), F32),
            pltpu.VMEM((1, ELEM), F32),
        ),
        in_specs=[hbm] * len(arrays),
        out_specs=(vmem, vmem),
        scratch_shapes=[
            pltpu.VMEM((1, ELEM), jnp.int32),
            pltpu.VMEM((1, ELEM), jnp.int32),
            pltpu.VMEM((1, ELEM), jnp.int32),
            pltpu.VMEM((NV, MODES, ELEM), F32),
            pltpu.VMEM((P1, P1, 3, ELEM), F32),
            pltpu.VMEM((NV, MODES, ELEM), F32),
            pltpu.VMEM((6, ELEM), jnp.int32),
            pltpu.VMEM(tangents.shape, BF16),
            pltpu.VMEM(vol_u.shape, BF16),
            pltpu.VMEM(vol_p.shape, BF16),
            pltpu.VMEM(face_u.shape, BF16),
            pltpu.VMEM(face_p.shape, BF16),
            pltpu.VMEM((GRP, BLOCK, MPAD), F32),
            pltpu.VMEM((SLOTS, ELEM), BF16),
            pltpu.VMEM((MPAD, ELEM), jnp.int32),
            pltpu.VMEM((MPAD, ELEM), F32),
            pltpu.VMEM((80, ELEM), F32),
            pltpu.VMEM((2 * NV, 8, ELEM), F32),
            pltpu.VMEM((NV, KCAT, ELEM), BF16),
            pltpu.VMEM((NV, KCAT, ELEM), BF16),
            pltpu.VMEM((2, NV * TM, ELEM), F32),
            pltpu.VMEM((6, NV * TM, ELEM), F32),
            pltpu.VMEM((6, NV, PT, ELEM), F32),
            pltpu.VMEM((6, NV, PT, ELEM), F32),
            pltpu.VMEM((NV, 4 * PT, ELEM), F32),
            pltpu.VMEM((NV, 176, ELEM), F32),
            pltpu.VMEM((8, ELEM), F32),
            pltpu.VMEM((3 * TM, NV * ELEM), BF16),
            pltpu.VMEM((LEAF, 8, 128), F32),
            pltpu.VMEM((ROWS, 8, 128), F32),
            pltpu.VMEM((GRP, 8, 128), F32),
            dma((12,)),
            dma,
            dma((copies,)),
            dma((copies,)),
            dma((2,)),
            dma((2,)),
            dma((LEAF,)),
            dma((LEAF,)),
            dma((ROWS,)),
            dma((ROWS,)),
            dma((GRP,)),
            dma((GRP,)),
            pltpu.SemaphoreType.REGULAR((3,)),
            pltpu.SemaphoreType.REGULAR((4,)),
        ],
        compiler_params=pltpu.CompilerParams(
            collective_id=0, has_side_effects=True, vmem_limit_bytes=32 << 20
        ),
    )(*[pltpu.with_memory_space_constraint(x, pltpu.HBM) for x in arrays])
    moved_state, moved_adjoint, moved_factors, moved_order, share = pl.pallas_call(
        unpack,
        name="unpack_slots",
        out_shape=(
            jax.ShapeDtypeStruct((NV, MODES, SLOTS), F32),
            jax.ShapeDtypeStruct((NV, MODES, SLOTS), F32),
            jax.ShapeDtypeStruct((P1, P1, 3, SLOTS), F32),
            jax.ShapeDtypeStruct((1, SLOTS), jnp.int32),
            jax.ShapeDtypeStruct((1, ELEM), F32),
        ),
        in_specs=[vmem, vmem],
        out_specs=(hbm,) * 5,
        scratch_shapes=[
            pltpu.VMEM((COLS, MODES, SLOTS), F32),
            pltpu.VMEM((COLS, 8, SLOTS), F32),
            pltpu.VMEM((P1, P1, 3, SLOTS), F32),
            pltpu.VMEM((1, SLOTS), jnp.int32),
            dma((COLS + 3,)),
        ],
        compiler_params=pltpu.CompilerParams(vmem_limit_bytes=24 << 20),
    )(*[pltpu.with_memory_space_constraint(x, pltpu.VMEM) for x in (recv, share)])
    return (
        share.reshape(ELEM),
        moved_state,
        moved_adjoint,
        moved_factors.transpose(2, 0, 1, 3),
        moved_order.reshape(SLOTS),
    )


def solution(mesh):
    return jax.shard_map(
        body,
        mesh=mesh,
        in_specs=(
            P(None, None, ("grp", "dom")),
            P(None, None, ("grp", "dom")),
            P(None, None, None, ("grp", "dom")),
            P(("grp", "dom")),
            P(("grp", "dom")),
            P(None, ("grp", "dom")),
            P(("grp", "dom"), None),
        ),
        out_specs=(
            P(("grp", "dom")),
            P(None, None, ("grp", "dom")),
            P(None, None, ("grp", "dom")),
            P(None, None, None, ("grp", "dom")),
            P(("grp", "dom")),
        ),
        check_vma=False,
    )
```

```python
import functools
import math

import jax
import jax.numpy as jnp
import ml_dtypes
import numpy as np
from jax import lax
from jax.experimental import pallas as pl
from jax.experimental.pallas import tpu as pltpu
from jax.sharding import PartitionSpec as P

NV = 6
PMAX = 4
P1 = 5
MODES = 125
NQ1 = 7
ELEM = 256
CAP = 24
GRP = 16
DOM = 32
SLOTS = GRP * CAP
LEAF = 8
ROWS = DOM // LEAF
MPAD = 128
PT = 56
TM = 32
KCAT = 3 * MPAD
FROWS = 3 * P1 * P1 + 1
SPARE = MPAD - MODES
REST = FROWS - 2 * NV * SPARE
REST_AT = 2 * NV * SPARE % 8
MESH = pl.DeviceIdType.MESH
COLS = 2 * NV
BLOCK = COLS * CAP + 8
PIECES = ((0, 1), (1, 2), (3, 3), (6, 3), (9, 3))
NEAR = 2
FIRST = (3, 8)
LATER = ((7,), (6,), (5, 4))
F32 = jnp.float32
BF16 = jnp.bfloat16


def line_tables():
    place = math.pi * (np.arange(NQ1) + 0.5) / NQ1
    points = -np.cos(place)
    weights = math.pi / NQ1 * np.sin(place)
    values = [np.ones(NQ1), points]
    slopes = [np.zeros(NQ1), np.ones(NQ1)]
    for n in range(1, P1 - 1):
        values.append(((2 * n + 1) * points * values[n] - n * values[n - 1]) / (n + 1))
        slopes.append(slopes[n - 1] + (2 * n + 1) * values[n])
    norm = np.sqrt((2 * np.arange(P1) + 1) / 2.0)
    vt = np.stack(values, axis=1) * norm
    st = np.stack(slopes, axis=1) * norm
    ends = [norm * (-1.0) ** np.arange(P1), norm]
    return vt, st, ends, weights


def split(table):
    high = table.astype(np.float32).astype(ml_dtypes.bfloat16)
    low = (table - high.astype(np.float64)).astype(np.float32).astype(ml_dtypes.bfloat16)
    return high, low


def against_split(table):
    rows, depth = table.shape
    pad = MPAD if depth == MODES else TM
    high, low = split(table)
    out = np.zeros((rows, 3 * pad), ml_dtypes.bfloat16)
    out[:, :depth] = high
    out[:, pad : pad + depth] = high
    out[:, 2 * pad : 2 * pad + depth] = low
    return out


def padded(table, rows):
    return np.concatenate([table, np.zeros((rows - table.shape[0],) + table.shape[1:])])


def tables():
    vt, st, ends, w = line_tables()

    def plane(a, first, second, third):
        return np.einsum("i,bj,ck->bcijk", first[a], second, third).reshape(NQ1 * NQ1, MODES)

    face_w = np.outer(w, w).reshape(-1, 1)
    vol_u, vol_p = [], []
    for a in range(NQ1):
        grads = [plane(a, st, vt, vt), plane(a, vt, st, vt), plane(a, vt, vt, st)]
        vol_u.append(np.concatenate([padded(t, PT) for t in [plane(a, vt, vt, vt)] + grads]))
        vol_p.append(padded(np.concatenate([padded(w[a] * face_w * t, PT) for t in grads]), 176))
    eye = np.eye(P1)

    def face(f, tangent):
        e = ends[f % 2][None]
        parts = [e, tangent, tangent] if f < 2 else [tangent, e, tangent] if f < 4 else [tangent, tangent, e]
        out = np.einsum("ai,bj,ck->abcijk", *parts)
        return out.reshape(-1, MODES)

    modal = [padded(face(f, eye), TM) for f in (1, 0, 3, 2, 5, 4)]
    at_points = [padded(face(f, vt), PT) for f in range(6)]
    weighted = [padded(face_w * face(f, vt), PT) for f in range(6)]
    face_u = np.concatenate(modal + at_points)
    face_p = np.concatenate(weighted)
    tangents = padded(np.einsum("bj,ck->bcjk", vt, vt).reshape(NQ1 * NQ1, P1 * P1), 64)
    return (
        np.stack([against_split(t) for t in vol_u]),
        np.stack([against_split(t) for t in vol_p]),
        against_split(face_u),
        against_split(face_p),
        against_split(tangents),
    )


def dot(a, b):
    return lax.dot_general(a, b, (((1,), (0,)), ((), ())), preferred_element_type=F32)


def dot_rows(a, b):
    return lax.dot_general(a, b, (((1,), (1,)), ((), ())), preferred_element_type=F32)


def halves(x):
    high = x.astype(BF16)
    return high, (x - high.astype(F32)).astype(BF16)


def thirds(x):
    high = x.astype(BF16)
    rest = x - high.astype(F32)
    mid = rest.astype(BF16)
    return high, mid, (rest - mid.astype(F32)).astype(BF16)


def digit_sum(m, step, count):
    total = jnp.zeros(m.shape, jnp.int32)
    for n in range(1, count):
        total = total + jnp.where(m >= n * step, 1, 0)
    return total


def top_of(rows):
    m = lax.broadcasted_iota(jnp.int32, (rows, ELEM), 0)
    i = digit_sum(m, P1 * P1, P1)
    m = m - i * (P1 * P1)
    j = digit_sum(m, P1, P1)
    k = m - j * P1
    return jnp.maximum(jnp.maximum(i, j), k)


def factor_top(rows):
    m = lax.broadcasted_iota(jnp.int32, (rows, ELEM), 0)
    i = digit_sum(m, 3 * P1, P1)
    j = digit_sum(m - i * (3 * P1), 3, P1)
    return jnp.maximum(i, j)


def speed(values, lead):
    return lead * lax.rsqrt(1.0 + values * values)


def work(
    state_hbm,
    adjoint_hbm,
    factors_hbm,
    order_hbm,
    marks_hbm,
    neighbours_hbm,
    owner_hbm,
    vol_u_hbm,
    vol_p_hbm,
    face_u_hbm,
    face_p_hbm,
    tangents_hbm,
    recv,
    share,
    owner,
    order,
    marks,
    state,
    factors,
    adjoint,
    neighbours,
    tangents,
    vol_u,
    vol_p,
    face_u,
    face_p,
    send,
    sel,
    top,
    padded_x,
    fac,
    fac3,
    us,
    ps,
    hsend,
    outer,
    own,
    own_p,
    vals,
    vals_p,
    near,
    gath,
    leaf_sum,
    row_sum,
    grp_sum,
    load_sem,
    self_sem,
    send_sem,
    recv_sem,
    halo_send,
    halo_recv,
    leaf_send,
    leaf_recv,
    row_send,
    row_recv,
    sum_send,
    sum_recv,
    grp_in,
    dom_in,
):
    g = lax.axis_index("grp")
    r = lax.axis_index("dom")
    lane = lax.rem(r, LEAF)
    row = r // LEAF
    after = lax.rem(r + 1, DOM)
    before = lax.rem(r + DOM - 1, DOM)

    barrier = pltpu.get_barrier_semaphore()

    def greet(to_g, to_r):
        pl.semaphore_signal(barrier, inc=1, device_id=(to_g, to_r), device_id_type=MESH)

    greet(lax.rem(g + 1, GRP), r)
    greet(lax.rem(g + GRP - 1, GRP), r)
    greet(g, after)
    greet(g, before)
    greeted = 4

    def tell_grp(n):
        for to_g in (lax.rem(g + 2**n, GRP), lax.rem(g + GRP - 2**n, GRP)):
            pl.semaphore_signal(
                grp_in.at[n], inc=1, device_id=(to_g, r), device_id_type=MESH
            )

    def tell_dom(n):
        for to_r in (lax.rem(r + 2**n, DOM), lax.rem(r + DOM - 2**n, DOM)):
            pl.semaphore_signal(
                dom_in.at[n], inc=1, device_id=(g, to_r), device_id_type=MESH
            )

    def told_dom(n):
        pl.semaphore_wait(dom_in.at[n], 2)
        if n < 3:
            tell_dom(n + 1)

    def told_grp(n):
        pl.semaphore_wait(grp_in.at[n], 2)
        if n < 2:
            tell_grp(n + 1)

    loads = [
        pltpu.make_async_copy(source, target, load_sem.at[n])
        for n, (source, target) in enumerate(
            (
                (owner_hbm, owner),
                (order_hbm, order),
                (marks_hbm, marks),
                (factors_hbm, factors),
                (state_hbm, state),
                (adjoint_hbm, adjoint),
                (face_u_hbm, face_u),
                (neighbours_hbm, neighbours),
                (tangents_hbm, tangents),
                (vol_u_hbm, vol_u),
                (vol_p_hbm, vol_p),
                (face_p_hbm, face_p),
            )
        )
    ]
    for load in loads:
        load.start()

    top[...] = top_of(MPAD)
    loads[0].wait()
    to = owner[...]
    hits = jnp.where(lax.broadcasted_iota(jnp.int32, (GRP, ELEM), 0) == to, 1.0, 0.0)
    earlier = jnp.where(
        lax.broadcasted_iota(jnp.int32, (ELEM, ELEM), 0)
        < lax.broadcasted_iota(jnp.int32, (ELEM, ELEM), 1),
        1.0,
        0.0,
    ).astype(BF16)
    counts = dot(hits.astype(BF16), earlier)
    rank = jnp.sum(hits * counts, axis=0, keepdims=True).astype(jnp.int32)
    slot = to * CAP + rank
    sel[...] = jnp.where(
        lax.broadcasted_iota(jnp.int32, (SLOTS, ELEM), 0) == slot, 1.0, 0.0
    ).astype(BF16)

    for load in loads[1:4]:
        load.wait()
    level = order[...]
    fresh = jnp.clip(level + marks[...], 1, PMAX)
    low = jnp.minimum(level, fresh)

    for i in range(P1):
        for j in range(P1):
            at = (i * P1 + j) * 3
            fac[at : at + 3, :] = factors[i, j]
    fac[FROWS - 1 : 80, :] = jnp.zeros((80 - FROWS + 1, ELEM), F32)
    rows = lax.broadcasted_iota(jnp.int32, (80, ELEM), 0)
    kept = jnp.where(factor_top(80) <= low, fac[...], 0.0)
    fac[...] = jnp.where(rows == FROWS - 1, fresh.astype(F32), kept)
    for n in range(2 * NV):
        fac3[n, 0:SPARE, :] = fac[n * SPARE : (n + 1) * SPARE, :]

    def pack(source, v, most, column):
        padded_x[0:MODES, :] = jnp.where(top[0:MODES, :] <= most, source[v], 0.0)
        padded_x[MODES:MPAD, :] = fac3[column, 0:SPARE, :]
        high, mid, tail = thirds(padded_x[...])
        chosen = sel[...]
        out = dot_rows(chosen, tail) + dot_rows(chosen, mid) + dot_rows(chosen, high)
        place = pl.ds(pl.multiple_of(column * CAP, 8), CAP)
        send[:, place, :] = out.reshape(GRP, CAP, MPAD)

    def pack_rest():
        total = jnp.zeros((GRP * 8, MPAD), F32)
        line = lax.broadcasted_iota(jnp.int32, (GRP * 8, ELEM), 0)
        line_slot = (line // 8) * CAP + lax.rem(line, 8)
        from_row = 2 * NV * SPARE - REST_AT
        rest = fac[from_row : from_row + REST + 8, :]
        rest = jnp.concatenate([rest, jnp.zeros((MPAD - REST - 8, ELEM), F32)], axis=0)
        rest = jnp.where(lax.broadcasted_iota(jnp.int32, (MPAD, ELEM), 0) < REST_AT, 0.0, rest)
        for part in range(3):
            chosen = jnp.where(line_slot + 8 * part == slot, 1.0, 0.0).astype(BF16)
            moved = rest if part == 0 else pltpu.roll(rest, REST * part, 0)
            for piece in reversed(thirds(moved)):
                total = total + dot_rows(chosen, piece)
        send[:, COLS * CAP : BLOCK, :] = total.reshape(GRP, 8, MPAD)

    def block_to(ahead, n, first, count):
        to_g = lax.rem(g + ahead + GRP, GRP)
        rows = pl.ds(first, count)
        return pltpu.make_async_remote_copy(
            src_ref=send.at[to_g, rows],
            dst_ref=recv.at[g, rows],
            send_sem=send_sem.at[n],
            recv_sem=recv_sem.at[n],
            device_id=(to_g, r),
            device_id_type=MESH,
        )

    partners = [k for d in range(1, GRP // 2) for k in (d, -d)] + [GRP // 2]
    blocks = {}
    for k in partners:
        n = len(blocks) if not blocks else max(blocks.values(), key=lambda x: x[-1][1])[-1][1] + 1
        if abs(k) <= NEAR:
            cut = [0] + [(c + count) * CAP for c, count in PIECES[:-1]] + [BLOCK]
            blocks[k] = [(p, n + p, cut[p], cut[p + 1] - cut[p]) for p in range(len(PIECES))]
        else:
            blocks[k] = [(0, n, 0, BLOCK)]

    def send_block(k, p=0):
        block_to(k, *blocks[k][p][1:]).start()

    def send_piece(p, distance):
        send_block(distance, p)
        send_block(-distance, p)

    own_block = pltpu.make_async_copy(send.at[g], recv.at[g], self_sem)

    def pack_columns(first, count):
        @pl.loop(first, min(first + count, NV))
        def _(c):
            pack(state, c, low, c)

        @pl.loop(max(first, NV), first + count)
        def _(c):
            pack(adjoint, c - NV, fresh, c)

    loads[4].wait()
    for p, (first, count) in enumerate(PIECES):
        if first <= NV < first + count or first == NV:
            loads[5].wait()
        pack_columns(first, count)
        if p == 0:
            pl.semaphore_wait(barrier, greeted)
            tell_grp(0)
            tell_dom(0)
        if p == len(PIECES) - 1:
            pack_rest()
        send_piece(p, 1)
        if p == 0:
            told_grp(0)
        send_piece(p, 2)
    told_grp(1)

    def send_far(distances):
        for d in distances:
            send_block(d)
            if 2 * d != GRP:
                send_block(-d)

    send_far(FIRST[:1])
    told_grp(2)
    send_far(FIRST[1:])
    own_block.start()
    told_dom(0)

    def split_into(target, source, v, most):
        padded_x[0:MODES, :] = jnp.where(top[0:MODES, :] <= most, source[v], 0.0)
        padded_x[MODES:MPAD, :] = jnp.zeros((SPARE, ELEM), F32)
        high, tail = halves(padded_x[...])
        target[v, 0:MPAD, :] = high
        target[v, MPAD : 2 * MPAD, :] = tail
        target[v, 2 * MPAD :, :] = high

    loads[6].wait()

    @pl.loop(0, NV)
    def _(v):
        split_into(us, state, v, level)
        both = dot(face_u[...], us[v])
        place = pl.ds(pl.multiple_of(v * TM, TM), TM)
        for b in range(4):
            outer[b, place, :] = both[b * TM : (b + 1) * TM]
        hsend[0, place, :] = both[4 * TM : 5 * TM]
        hsend[1, place, :] = both[5 * TM : 6 * TM]
        for f in range(6):
            own[f, v] = both[6 * TM + f * PT : 6 * TM + (f + 1) * PT]

    halos = [
        pltpu.make_async_remote_copy(
            src_ref=hsend.at[n],
            dst_ref=outer.at[4 + n],
            send_sem=halo_send.at[n],
            recv_sem=halo_recv.at[n],
            device_id=(g, to_r),
            device_id_type=MESH,
        )
        for n, to_r in enumerate((after, before))
    ]
    for halo in halos:
        halo.start()
    told_dom(1)

    @pl.loop(0, NV)
    def _(v):
        split_into(ps, adjoint, v, level + 1)

    told_dom(2)
    loads[9].wait()
    loads[10].wait()
    near[...] = jnp.zeros(near.shape, F32)

    @pl.loop(0, NQ1)
    def _(a):
        @pl.loop(0, NV)
        def _(v):
            vals[v] = dot(vol_u[a], us[v])
            vals_p[v] = dot(vol_p[a], ps[v])

        @pl.loop(0, PT // 8)
        def _(t):
            def at(table, v):
                return vals[v, pl.ds(pl.multiple_of(table * PT + t * 8, 8), 8), :]

            def at_p(table, v):
                return vals_p[v, pl.ds(pl.multiple_of(table * PT + t * 8, 8), 8), :]

            u0 = at(0, 0)
            inverse = lax.rsqrt(1.0 + u0 * u0)
            c = [at(0, 1 + d) * inverse for d in range(3)]
            u5 = at(0, 5)
            soft = jnp.maximum(u5, 0.0) + jnp.log1p(jnp.exp(-jnp.abs(u5)))
            nu = 0.05 + 0.1 * soft
            total = jnp.zeros((8, ELEM), F32)
            for v in range(NV):
                w = [at_p(d, v) for d in range(3)]
                carried = w[0] * c[0] + w[1] * c[1] + w[2] * c[2]
                spread = w[0] * at(1, v) + w[1] * at(2, v) + w[2] * at(3, v)
                total = total + (carried * at(0, v) - nu * spread)
            near[...] = near[...] - total

    loads[11].wait()
    loads[7].wait()
    loads[8].wait()

    @pl.loop(0, NV)
    def _(v):
        both = dot(face_p[...], ps[v])
        for f in range(6):
            own_p[f, v] = both[f * PT : (f + 1) * PT]

    for halo in halos:
        halo.wait()
    told_dom(3)

    @pl.loop(0, 6)
    def _(f):
        absent = jnp.where(f == 4, jnp.where(r == 0, 1, 0), 0) + jnp.where(
            f == 5, jnp.where(r == DOM - 1, 1, 0), 0
        )
        present = 1.0 - absent.astype(F32)
        high, tail = halves(outer[f] * present)
        source = lax.broadcasted_iota(jnp.int32, (ELEM, ELEM), 0)
        pick = jnp.where(source == neighbours[pl.ds(f, 1), :], 1.0, 0.0).astype(BF16)
        got_high = dot(high, pick).astype(BF16)
        got_tail = dot(tail, pick).astype(BF16)
        for v in range(NV):
            lanes = slice(v * ELEM, (v + 1) * ELEM)
            gath[0:TM, lanes] = got_high[v * TM : (v + 1) * TM]
            gath[TM : 2 * TM, lanes] = got_tail[v * TM : (v + 1) * TM]
            gath[2 * TM :, lanes] = got_high[v * TM : (v + 1) * TM]
        seen = dot(tangents[...], gath[...])
        o = [seen[0:PT, v * ELEM : (v + 1) * ELEM] for v in range(NV)]
        d = f // 2
        sign = (2 * lax.rem(f, 2) - 1).astype(F32)
        lead_o = jnp.where(d == 0, o[1], jnp.where(d == 1, o[2], o[3]))
        half = 0.5 * sign
        speed_t = half * speed(own[f, 0], own[f, 1 + d])
        speed_o = half * speed(o[0], lead_o)
        total = jnp.zeros((PT, ELEM), F32)
        for v in range(NV):
            t = own[f, v]
            total = total + own_p[f, v] * (
                speed_t * t + speed_o * o[v] + 0.5 * (t - o[v])
            )
        part = total[0:8]
        for n in range(1, PT // 8):
            part = part + total[n * 8 : (n + 1) * 8]
        near[...] = near[...] + part

    eta = jnp.abs(jnp.sum(near[...], axis=0, keepdims=True))

    def exchange(buffer, mine, count, send_s, recv_s, device, then):
        def one(k):
            return pltpu.make_async_remote_copy(
                src_ref=buffer.at[mine],
                dst_ref=buffer.at[mine],
                send_sem=send_s.at[k],
                recv_sem=recv_s.at[k],
                device_id=device(k),
                device_id_type=MESH,
            )

        @pl.loop(1, count)
        def _(k):
            one(k).start()

        send_far(then)

        @pl.loop(1, count)
        def _(k):
            one(k).wait()

        return jnp.sum(buffer[...], axis=0)

    leaf_sum[lane] = jnp.broadcast_to(jnp.sum(eta, axis=1, keepdims=True), (8, 128))
    part = exchange(
        leaf_sum, lane, LEAF, leaf_send, leaf_recv,
        lambda k: (g, row * LEAF + lax.rem(lane + k, LEAF)),
        LATER[0],
    )
    row_sum[row] = part
    part = exchange(
        row_sum, row, ROWS, row_send, row_recv,
        lambda k: (g, lax.rem(row + k, ROWS) * LEAF + lane),
        LATER[1],
    )
    grp_sum[g] = part
    part = exchange(
        grp_sum, g, GRP, sum_send, sum_recv, lambda k: (lax.rem(g + k, GRP), r),
        LATER[2],
    )
    mean = part[0:1, 0:1] / (ELEM * GRP * DOM)
    share[...] = eta / (mean + 1e-06)

    own_block.wait()
    for k in partners:
        for piece in blocks[k]:
            block_to(k, *piece[1:]).wait()


def unpack(
    recv,
    share_in,
    moved_state,
    moved_adjoint,
    moved_factors,
    moved_order,
    share,
    columns,
    spare,
    factors,
    order,
    sem,
):
    copies = []

    def put(source, target):
        copy = pltpu.make_async_copy(source, target, sem.at[len(copies)])
        copy.start()
        copies.append(copy)

    put(share_in, share)
    for c in range(COLS):
        lines = recv[:, c * CAP : (c + 1) * CAP, :].reshape(SLOTS, MPAD).T
        columns[c] = lines[0:MODES]
        spare[c, 0:SPARE, :] = lines[MODES:MPAD]
        target = moved_state.at[c] if c < NV else moved_adjoint.at[c - NV]
        put(columns.at[c], target)
    rest = recv[:, COLS * CAP : BLOCK, :].reshape(GRP * 8, MPAD)
    parts = [rest] + [pltpu.roll(rest, MPAD - REST * n, 1) for n in (1, 2)]
    parts = [part.reshape(GRP, 1, 8, MPAD) for part in parts]
    lines = jnp.concatenate(parts, axis=1).reshape(SLOTS, MPAD).T
    rows = [spare[c, 0:SPARE, :] for c in range(COLS)]
    whole = jnp.concatenate(rows + [lines[REST_AT : REST_AT + REST]], axis=0)
    for i in range(P1):
        for j in range(P1):
            at = (i * P1 + j) * 3
            factors[i, j] = whole[at : at + 3]
    put(factors, moved_factors)
    order[...] = whole[FROWS - 1 : FROWS].astype(jnp.int32).reshape(SLOTS)
    put(order, moved_order)
    for copy in copies:
        copy.wait()


def body(state, adjoint, factors, order, marks, neighbours, new_owner):
    vol_u, vol_p, face_u, face_p, tangents = [jnp.asarray(t) for t in tables()]
    hbm = pl.BlockSpec(memory_space=pltpu.HBM)
    vmem = pl.BlockSpec(memory_space=pltpu.VMEM)
    dma = pltpu.SemaphoreType.DMA
    copies = GRP - 1 + 2 * NEAR * (len(PIECES) - 1)
    arrays = (
        state,
        adjoint,
        factors.transpose(1, 2, 0, 3),
        order.reshape(1, ELEM),
        marks.reshape(1, ELEM),
        neighbours,
        new_owner.reshape(1, ELEM),
        vol_u,
        vol_p,
        face_u,
        face_p,
        tangents,
    )
    recv, share = pl.pallas_call(
        work,
        name="indicator_and_send",
        out_shape=(
            pltpu.VMEM((GRP, BLOCK, MPAD), F32),
            pltpu.VMEM((1, ELEM), F32),
        ),
        in_specs=[hbm] * len(arrays),
        out_specs=(vmem, vmem),
        scratch_shapes=[
            pltpu.VMEM((1, ELEM), jnp.int32),
            pltpu.VMEM((1, ELEM), jnp.int32),
            pltpu.VMEM((1, ELEM), jnp.int32),
            pltpu.VMEM((NV, MODES, ELEM), F32),
            pltpu.VMEM((P1, P1, 3, ELEM), F32),
            pltpu.VMEM((NV, MODES, ELEM), F32),
            pltpu.VMEM((6, ELEM), jnp.int32),
            pltpu.VMEM(tangents.shape, BF16),
            pltpu.VMEM(vol_u.shape, BF16),
            pltpu.VMEM(vol_p.shape, BF16),
            pltpu.VMEM(face_u.shape, BF16),
            pltpu.VMEM(face_p.shape, BF16),
            pltpu.VMEM((GRP, BLOCK, MPAD), F32),
            pltpu.VMEM((SLOTS, ELEM), BF16),
            pltpu.VMEM((MPAD, ELEM), jnp.int32),
            pltpu.VMEM((MPAD, ELEM), F32),
            pltpu.VMEM((80, ELEM), F32),
            pltpu.VMEM((2 * NV, 8, ELEM), F32),
            pltpu.VMEM((NV, KCAT, ELEM), BF16),
            pltpu.VMEM((NV, KCAT, ELEM), BF16),
            pltpu.VMEM((2, NV * TM, ELEM), F32),
            pltpu.VMEM((6, NV * TM, ELEM), F32),
            pltpu.VMEM((6, NV, PT, ELEM), F32),
            pltpu.VMEM((6, NV, PT, ELEM), F32),
            pltpu.VMEM((NV, 4 * PT, ELEM), F32),
            pltpu.VMEM((NV, 176, ELEM), F32),
            pltpu.VMEM((8, ELEM), F32),
            pltpu.VMEM((3 * TM, NV * ELEM), BF16),
            pltpu.VMEM((LEAF, 8, 128), F32),
            pltpu.VMEM((ROWS, 8, 128), F32),
            pltpu.VMEM((GRP, 8, 128), F32),
            dma((12,)),
            dma,
            dma((copies,)),
            dma((copies,)),
            dma((2,)),
            dma((2,)),
            dma((LEAF,)),
            dma((LEAF,)),
            dma((ROWS,)),
            dma((ROWS,)),
            dma((GRP,)),
            dma((GRP,)),
            pltpu.SemaphoreType.REGULAR((3,)),
            pltpu.SemaphoreType.REGULAR((4,)),
        ],
        compiler_params=pltpu.CompilerParams(
            collective_id=0, has_side_effects=True, vmem_limit_bytes=32 << 20
        ),
    )(*[pltpu.with_memory_space_constraint(x, pltpu.HBM) for x in arrays])
    moved_state, moved_adjoint, moved_factors, moved_order, share = pl.pallas_call(
        unpack,
        name="unpack_slots",
        out_shape=(
            jax.ShapeDtypeStruct((NV, MODES, SLOTS), F32),
            jax.ShapeDtypeStruct((NV, MODES, SLOTS), F32),
            jax.ShapeDtypeStruct((P1, P1, 3, SLOTS), F32),
            jax.ShapeDtypeStruct((SLOTS,), jnp.int32),
            jax.ShapeDtypeStruct((1, ELEM), F32),
        ),
        in_specs=[vmem, vmem],
        out_specs=(hbm,) * 5,
        scratch_shapes=[
            pltpu.VMEM((COLS, MODES, SLOTS), F32),
            pltpu.VMEM((COLS, 8, SLOTS), F32),
            pltpu.VMEM((P1, P1, 3, SLOTS), F32),
            pltpu.VMEM((SLOTS,), jnp.int32),
            dma((COLS + 3,)),
        ],
        compiler_params=pltpu.CompilerParams(vmem_limit_bytes=24 << 20),
    )(*[pltpu.with_memory_space_constraint(x, pltpu.VMEM) for x in (recv, share)])
    return (
        share.reshape(ELEM),
        moved_state,
        moved_adjoint,
        moved_factors.transpose(2, 0, 1, 3),
        moved_order,
    )


def solution(mesh):
    return jax.shard_map(
        body,
        mesh=mesh,
        in_specs=(
            P(None, None, ("grp", "dom")),
            P(None, None, ("grp", "dom")),
            P(None, None, None, ("grp", "dom")),
            P(("grp", "dom")),
            P(("grp", "dom")),
            P(None, ("grp", "dom")),
            P(("grp", "dom"), None),
        ),
        out_specs=(
            P(("grp", "dom")),
            P(None, None, ("grp", "dom")),
            P(None, None, ("grp", "dom")),
            P(None, None, None, ("grp", "dom")),
            P(("grp", "dom")),
        ),
        check_vma=False,
    )
```

```python
import functools
import math

import jax
import jax.numpy as jnp
import ml_dtypes
import numpy as np
from jax import lax
from jax.experimental import pallas as pl
from jax.experimental.pallas import tpu as pltpu
from jax.sharding import PartitionSpec as P

NV = 6
PMAX = 4
P1 = 5
MODES = 125
NQ1 = 7
ELEM = 256
CAP = 24
GRP = 16
DOM = 32
SLOTS = GRP * CAP
LEAF = 8
ROWS = DOM // LEAF
MPAD = 128
PT = 56
TM = 32
KCAT = 3 * MPAD
FROWS = 3 * P1 * P1 + 1
SPARE = MPAD - MODES
REST = FROWS - 2 * NV * SPARE
REST_AT = 2 * NV * SPARE % 8
MESH = pl.DeviceIdType.MESH
COLS = 2 * NV
BLOCK = COLS * CAP + 8
PIECES = ((0, 1), (1, 1), (2, 2), (4, 2), (6, 3), (9, 3))
NEAR = 2
FIRST = (3, 8)
LATER = ((7,), (6,), (5, 4))
F32 = jnp.float32
BF16 = jnp.bfloat16


def line_tables():
    place = math.pi * (np.arange(NQ1) + 0.5) / NQ1
    points = -np.cos(place)
    weights = math.pi / NQ1 * np.sin(place)
    values = [np.ones(NQ1), points]
    slopes = [np.zeros(NQ1), np.ones(NQ1)]
    for n in range(1, P1 - 1):
        values.append(((2 * n + 1) * points * values[n] - n * values[n - 1]) / (n + 1))
        slopes.append(slopes[n - 1] + (2 * n + 1) * values[n])
    norm = np.sqrt((2 * np.arange(P1) + 1) / 2.0)
    vt = np.stack(values, axis=1) * norm
    st = np.stack(slopes, axis=1) * norm
    ends = [norm * (-1.0) ** np.arange(P1), norm]
    return vt, st, ends, weights


def split(table):
    high = table.astype(np.float32).astype(ml_dtypes.bfloat16)
    low = (table - high.astype(np.float64)).astype(np.float32).astype(ml_dtypes.bfloat16)
    return high, low


def against_split(table):
    rows, depth = table.shape
    pad = MPAD if depth == MODES else TM
    high, low = split(table)
    out = np.zeros((rows, 3 * pad), ml_dtypes.bfloat16)
    out[:, :depth] = high
    out[:, pad : pad + depth] = high
    out[:, 2 * pad : 2 * pad + depth] = low
    return out


def padded(table, rows):
    return np.concatenate([table, np.zeros((rows - table.shape[0],) + table.shape[1:])])


def tables():
    vt, st, ends, w = line_tables()

    def plane(a, first, second, third):
        return np.einsum("i,bj,ck->bcijk", first[a], second, third).reshape(NQ1 * NQ1, MODES)

    face_w = np.outer(w, w).reshape(-1, 1)
    vol_u, vol_p = [], []
    for a in range(NQ1):
        grads = [plane(a, st, vt, vt), plane(a, vt, st, vt), plane(a, vt, vt, st)]
        vol_u.append(np.concatenate([padded(t, PT) for t in [plane(a, vt, vt, vt)] + grads]))
        vol_p.append(padded(np.concatenate([padded(w[a] * face_w * t, PT) for t in grads]), 176))
    eye = np.eye(P1)

    def face(f, tangent):
        e = ends[f % 2][None]
        parts = [e, tangent, tangent] if f < 2 else [tangent, e, tangent] if f < 4 else [tangent, tangent, e]
        out = np.einsum("ai,bj,ck->abcijk", *parts)
        return out.reshape(-1, MODES)

    modal = [padded(face(f, eye), TM) for f in (1, 0, 3, 2, 5, 4)]
    at_points = [padded(face(f, vt), PT) for f in range(6)]
    weighted = [padded(face_w * face(f, vt), PT) for f in range(6)]
    face_u = np.concatenate(modal + at_points)
    face_p = np.concatenate(weighted)
    tangents = padded(np.einsum("bj,ck->bcjk", vt, vt).reshape(NQ1 * NQ1, P1 * P1), 64)
    return (
        np.stack([against_split(t) for t in vol_u]),
        np.stack([against_split(t) for t in vol_p]),
        against_split(face_u),
        against_split(face_p),
        against_split(tangents),
    )


def dot(a, b):
    return lax.dot_general(a, b, (((1,), (0,)), ((), ())), preferred_element_type=F32)


def dot_rows(a, b):
    return lax.dot_general(a, b, (((1,), (1,)), ((), ())), preferred_element_type=F32)


def halves(x):
    high = x.astype(BF16)
    return high, (x - high.astype(F32)).astype(BF16)


def thirds(x):
    high = x.astype(BF16)
    rest = x - high.astype(F32)
    mid = rest.astype(BF16)
    return high, mid, (rest - mid.astype(F32)).astype(BF16)


def digit_sum(m, step, count):
    total = jnp.zeros(m.shape, jnp.int32)
    for n in range(1, count):
        total = total + jnp.where(m >= n * step, 1, 0)
    return total


def top_of(rows):
    m = lax.broadcasted_iota(jnp.int32, (rows, ELEM), 0)
    i = digit_sum(m, P1 * P1, P1)
    m = m - i * (P1 * P1)
    j = digit_sum(m, P1, P1)
    k = m - j * P1
    return jnp.maximum(jnp.maximum(i, j), k)


def factor_top(rows):
    m = lax.broadcasted_iota(jnp.int32, (rows, ELEM), 0)
    i = digit_sum(m, 3 * P1, P1)
    j = digit_sum(m - i * (3 * P1), 3, P1)
    return jnp.maximum(i, j)


def speed(values, lead):
    return lead * lax.rsqrt(1.0 + values * values)


def work(
    state_hbm,
    adjoint_hbm,
    factors_hbm,
    order_hbm,
    marks_hbm,
    neighbours_hbm,
    owner_hbm,
    vol_u_hbm,
    vol_p_hbm,
    face_u_hbm,
    face_p_hbm,
    tangents_hbm,
    recv,
    share,
    owner,
    order,
    marks,
    state,
    factors,
    adjoint,
    neighbours,
    tangents,
    vol_u,
    vol_p,
    face_u,
    face_p,
    send,
    sel,
    top,
    padded_x,
    fac,
    fac3,
    us,
    ps,
    hsend,
    outer,
    own,
    own_p,
    vals,
    vals_p,
    near,
    gath,
    leaf_sum,
    row_sum,
    grp_sum,
    load_sem,
    self_sem,
    send_sem,
    recv_sem,
    halo_send,
    halo_recv,
    leaf_send,
    leaf_recv,
    row_send,
    row_recv,
    sum_send,
    sum_recv,
    grp_in,
    dom_in,
):
    g = lax.axis_index("grp")
    r = lax.axis_index("dom")
    lane = lax.rem(r, LEAF)
    row = r // LEAF
    after = lax.rem(r + 1, DOM)
    before = lax.rem(r + DOM - 1, DOM)

    barrier = pltpu.get_barrier_semaphore()

    def greet(to_g, to_r):
        pl.semaphore_signal(barrier, inc=1, device_id=(to_g, to_r), device_id_type=MESH)

    greet(lax.rem(g + 1, GRP), r)
    greet(lax.rem(g + GRP - 1, GRP), r)
    greet(g, after)
    greet(g, before)
    greeted = 4

    def tell_grp(n):
        for to_g in (lax.rem(g + 2**n, GRP), lax.rem(g + GRP - 2**n, GRP)):
            pl.semaphore_signal(
                grp_in.at[n], inc=1, device_id=(to_g, r), device_id_type=MESH
            )

    def tell_dom(n):
        for to_r in (lax.rem(r + 2**n, DOM), lax.rem(r + DOM - 2**n, DOM)):
            pl.semaphore_signal(
                dom_in.at[n], inc=1, device_id=(g, to_r), device_id_type=MESH
            )

    def told_dom(n):
        pl.semaphore_wait(dom_in.at[n], 2)
        if n < 3:
            tell_dom(n + 1)

    def told_grp(n):
        pl.semaphore_wait(grp_in.at[n], 2)
        if n < 2:
            tell_grp(n + 1)

    loads = [
        pltpu.make_async_copy(source, target, load_sem.at[n])
        for n, (source, target) in enumerate(
            (
                (owner_hbm, owner),
                (order_hbm, order),
                (marks_hbm, marks),
                (factors_hbm, factors),
                (state_hbm, state),
                (adjoint_hbm, adjoint),
                (face_u_hbm, face_u),
                (neighbours_hbm, neighbours),
                (tangents_hbm, tangents),
                (vol_u_hbm, vol_u),
                (vol_p_hbm, vol_p),
                (face_p_hbm, face_p),
            )
        )
    ]
    for load in loads:
        load.start()

    top[...] = top_of(MPAD)
    loads[0].wait()
    to = owner[...]
    hits = jnp.where(lax.broadcasted_iota(jnp.int32, (GRP, ELEM), 0) == to, 1.0, 0.0)
    earlier = jnp.where(
        lax.broadcasted_iota(jnp.int32, (ELEM, ELEM), 0)
        < lax.broadcasted_iota(jnp.int32, (ELEM, ELEM), 1),
        1.0,
        0.0,
    ).astype(BF16)
    counts = dot(hits.astype(BF16), earlier)
    rank = jnp.sum(hits * counts, axis=0, keepdims=True).astype(jnp.int32)
    slot = to * CAP + rank
    sel[...] = jnp.where(
        lax.broadcasted_iota(jnp.int32, (SLOTS, ELEM), 0) == slot, 1.0, 0.0
    ).astype(BF16)

    for load in loads[1:4]:
        load.wait()
    level = order[...]
    fresh = jnp.clip(level + marks[...], 1, PMAX)
    low = jnp.minimum(level, fresh)

    for i in range(P1):
        for j in range(P1):
            at = (i * P1 + j) * 3
            fac[at : at + 3, :] = factors[i, j]
    fac[FROWS - 1 : 80, :] = jnp.zeros((80 - FROWS + 1, ELEM), F32)
    rows = lax.broadcasted_iota(jnp.int32, (80, ELEM), 0)
    kept = jnp.where(factor_top(80) <= low, fac[...], 0.0)
    fac[...] = jnp.where(rows == FROWS - 1, fresh.astype(F32), kept)
    for n in range(2 * NV):
        fac3[n, 0:SPARE, :] = fac[n * SPARE : (n + 1) * SPARE, :]

    def pack(source, v, most, column):
        padded_x[0:MODES, :] = jnp.where(top[0:MODES, :] <= most, source[v], 0.0)
        padded_x[MODES:MPAD, :] = fac3[column, 0:SPARE, :]
        high, mid, tail = thirds(padded_x[...])
        chosen = sel[...]
        out = dot_rows(chosen, tail) + dot_rows(chosen, mid) + dot_rows(chosen, high)
        place = pl.ds(pl.multiple_of(column * CAP, 8), CAP)
        send[:, place, :] = out.reshape(GRP, CAP, MPAD)

    def pack_rest():
        total = jnp.zeros((GRP * 8, MPAD), F32)
        line = lax.broadcasted_iota(jnp.int32, (GRP * 8, ELEM), 0)
        line_slot = (line // 8) * CAP + lax.rem(line, 8)
        from_row = 2 * NV * SPARE - REST_AT
        rest = fac[from_row : from_row + REST + 8, :]
        rest = jnp.concatenate([rest, jnp.zeros((MPAD - REST - 8, ELEM), F32)], axis=0)
        rest = jnp.where(lax.broadcasted_iota(jnp.int32, (MPAD, ELEM), 0) < REST_AT, 0.0, rest)
        for part in range(3):
            chosen = jnp.where(line_slot + 8 * part == slot, 1.0, 0.0).astype(BF16)
            moved = rest if part == 0 else pltpu.roll(rest, REST * part, 0)
            for piece in reversed(thirds(moved)):
                total = total + dot_rows(chosen, piece)
        send[:, COLS * CAP : BLOCK, :] = total.reshape(GRP, 8, MPAD)

    def block_to(ahead, n, first, count):
        to_g = lax.rem(g + ahead + GRP, GRP)
        rows = pl.ds(first, count)
        return pltpu.make_async_remote_copy(
            src_ref=send.at[to_g, rows],
            dst_ref=recv.at[g, rows],
            send_sem=send_sem.at[n],
            recv_sem=recv_sem.at[n],
            device_id=(to_g, r),
            device_id_type=MESH,
        )

    partners = [k for d in range(1, GRP // 2) for k in (d, -d)] + [GRP // 2]
    blocks = {}
    for k in partners:
        n = len(blocks) if not blocks else max(blocks.values(), key=lambda x: x[-1][1])[-1][1] + 1
        if abs(k) <= NEAR:
            cut = [0] + [(c + count) * CAP for c, count in PIECES[:-1]] + [BLOCK]
            blocks[k] = [(p, n + p, cut[p], cut[p + 1] - cut[p]) for p in range(len(PIECES))]
        else:
            blocks[k] = [(0, n, 0, BLOCK)]

    def send_block(k, p=0):
        block_to(k, *blocks[k][p][1:]).start()

    def send_piece(p, distance):
        send_block(distance, p)
        send_block(-distance, p)

    own_block = pltpu.make_async_copy(send.at[g], recv.at[g], self_sem)

    def pack_columns(first, count):
        @pl.loop(first, min(first + count, NV))
        def _(c):
            pack(state, c, low, c)

        @pl.loop(max(first, NV), first + count)
        def _(c):
            pack(adjoint, c - NV, fresh, c)

    loads[4].wait()
    for p, (first, count) in enumerate(PIECES):
        if first <= NV < first + count or first == NV:
            loads[5].wait()
        pack_columns(first, count)
        if p == 0:
            pl.semaphore_wait(barrier, greeted)
            tell_grp(0)
            tell_dom(0)
        if p == len(PIECES) - 1:
            pack_rest()
        send_piece(p, 1)
        if p == 0:
            told_grp(0)
        send_piece(p, 2)
    told_grp(1)

    def send_far(distances):
        for d in distances:
            send_block(d)
            if 2 * d != GRP:
                send_block(-d)

    send_far(FIRST[:1])
    told_grp(2)
    send_far(FIRST[1:])
    own_block.start()
    told_dom(0)

    def split_into(target, source, v, most):
        padded_x[0:MODES, :] = jnp.where(top[0:MODES, :] <= most, source[v], 0.0)
        padded_x[MODES:MPAD, :] = jnp.zeros((SPARE, ELEM), F32)
        high, tail = halves(padded_x[...])
        target[v, 0:MPAD, :] = high
        target[v, MPAD : 2 * MPAD, :] = tail
        target[v, 2 * MPAD :, :] = high

    loads[6].wait()

    @pl.loop(0, NV)
    def _(v):
        split_into(us, state, v, level)
        both = dot(face_u[...], us[v])
        place = pl.ds(pl.multiple_of(v * TM, TM), TM)
        for b in range(4):
            outer[b, place, :] = both[b * TM : (b + 1) * TM]
        hsend[0, place, :] = both[4 * TM : 5 * TM]
        hsend[1, place, :] = both[5 * TM : 6 * TM]
        for f in range(6):
            own[f, v] = both[6 * TM + f * PT : 6 * TM + (f + 1) * PT]

    halos = [
        pltpu.make_async_remote_copy(
            src_ref=hsend.at[n],
            dst_ref=outer.at[4 + n],
            send_sem=halo_send.at[n],
            recv_sem=halo_recv.at[n],
            device_id=(g, to_r),
            device_id_type=MESH,
        )
        for n, to_r in enumerate((after, before))
    ]
    for halo in halos:
        halo.start()
    told_dom(1)

    @pl.loop(0, NV)
    def _(v):
        split_into(ps, adjoint, v, level + 1)

    told_dom(2)
    loads[9].wait()
    loads[10].wait()
    near[...] = jnp.zeros(near.shape, F32)

    @pl.loop(0, NQ1)
    def _(a):
        @pl.loop(0, NV)
        def _(v):
            vals[v] = dot(vol_u[a], us[v])
            vals_p[v] = dot(vol_p[a], ps[v])

        @pl.loop(0, PT // 8)
        def _(t):
            def at(table, v):
                return vals[v, pl.ds(pl.multiple_of(table * PT + t * 8, 8), 8), :]

            def at_p(table, v):
                return vals_p[v, pl.ds(pl.multiple_of(table * PT + t * 8, 8), 8), :]

            u0 = at(0, 0)
            inverse = lax.rsqrt(1.0 + u0 * u0)
            c = [at(0, 1 + d) * inverse for d in range(3)]
            u5 = at(0, 5)
            soft = jnp.maximum(u5, 0.0) + jnp.log1p(jnp.exp(-jnp.abs(u5)))
            nu = 0.05 + 0.1 * soft
            total = jnp.zeros((8, ELEM), F32)
            for v in range(NV):
                w = [at_p(d, v) for d in range(3)]
                carried = w[0] * c[0] + w[1] * c[1] + w[2] * c[2]
                spread = w[0] * at(1, v) + w[1] * at(2, v) + w[2] * at(3, v)
                total = total + (carried * at(0, v) - nu * spread)
            near[...] = near[...] - total

    loads[11].wait()
    loads[7].wait()
    loads[8].wait()

    @pl.loop(0, NV)
    def _(v):
        both = dot(face_p[...], ps[v])
        for f in range(6):
            own_p[f, v] = both[f * PT : (f + 1) * PT]

    for halo in halos:
        halo.wait()
    told_dom(3)

    @pl.loop(0, 6)
    def _(f):
        absent = jnp.where(f == 4, jnp.where(r == 0, 1, 0), 0) + jnp.where(
            f == 5, jnp.where(r == DOM - 1, 1, 0), 0
        )
        present = 1.0 - absent.astype(F32)
        high, tail = halves(outer[f] * present)
        source = lax.broadcasted_iota(jnp.int32, (ELEM, ELEM), 0)
        pick = jnp.where(source == neighbours[pl.ds(f, 1), :], 1.0, 0.0).astype(BF16)
        got_high = dot(high, pick).astype(BF16)
        got_tail = dot(tail, pick).astype(BF16)
        for v in range(NV):
            lanes = slice(v * ELEM, (v + 1) * ELEM)
            gath[0:TM, lanes] = got_high[v * TM : (v + 1) * TM]
            gath[TM : 2 * TM, lanes] = got_tail[v * TM : (v + 1) * TM]
            gath[2 * TM :, lanes] = got_high[v * TM : (v + 1) * TM]
        seen = dot(tangents[...], gath[...])
        o = [seen[0:PT, v * ELEM : (v + 1) * ELEM] for v in range(NV)]
        d = f // 2
        sign = (2 * lax.rem(f, 2) - 1).astype(F32)
        lead_o = jnp.where(d == 0, o[1], jnp.where(d == 1, o[2], o[3]))
        half = 0.5 * sign
        speed_t = half * speed(own[f, 0], own[f, 1 + d])
        speed_o = half * speed(o[0], lead_o)
        total = jnp.zeros((PT, ELEM), F32)
        for v in range(NV):
            t = own[f, v]
            total = total + own_p[f, v] * (
                speed_t * t + speed_o * o[v] + 0.5 * (t - o[v])
            )
        part = total[0:8]
        for n in range(1, PT // 8):
            part = part + total[n * 8 : (n + 1) * 8]
        near[...] = near[...] + part

    eta = jnp.abs(jnp.sum(near[...], axis=0, keepdims=True))

    def exchange(buffer, mine, count, send_s, recv_s, device, then):
        def one(k):
            return pltpu.make_async_remote_copy(
                src_ref=buffer.at[mine],
                dst_ref=buffer.at[mine],
                send_sem=send_s.at[k],
                recv_sem=recv_s.at[k],
                device_id=device(k),
                device_id_type=MESH,
            )

        @pl.loop(1, count)
        def _(k):
            one(k).start()

        send_far(then)

        @pl.loop(1, count)
        def _(k):
            one(k).wait()

        return jnp.sum(buffer[...], axis=0)

    leaf_sum[lane] = jnp.broadcast_to(jnp.sum(eta, axis=1, keepdims=True), (8, 128))
    part = exchange(
        leaf_sum, lane, LEAF, leaf_send, leaf_recv,
        lambda k: (g, row * LEAF + lax.rem(lane + k, LEAF)),
        LATER[0],
    )
    row_sum[row] = part
    part = exchange(
        row_sum, row, ROWS, row_send, row_recv,
        lambda k: (g, lax.rem(row + k, ROWS) * LEAF + lane),
        LATER[1],
    )
    grp_sum[g] = part
    part = exchange(
        grp_sum, g, GRP, sum_send, sum_recv, lambda k: (lax.rem(g + k, GRP), r),
        LATER[2],
    )
    mean = part[0:1, 0:1] / (ELEM * GRP * DOM)
    share[...] = eta / (mean + 1e-06)

    own_block.wait()
    for k in partners:
        for piece in blocks[k]:
            block_to(k, *piece[1:]).wait()


def unpack(
    recv,
    share_in,
    moved_state,
    moved_adjoint,
    moved_factors,
    moved_order,
    share,
    columns,
    spare,
    factors,
    order,
    sem,
):
    copies = []

    def put(source, target):
        copy = pltpu.make_async_copy(source, target, sem.at[len(copies)])
        copy.start()
        copies.append(copy)

    put(share_in, share)
    for c in range(COLS):
        lines = recv[:, c * CAP : (c + 1) * CAP, :].reshape(SLOTS, MPAD).T
        columns[c] = lines[0:MODES]
        spare[c, 0:SPARE, :] = lines[MODES:MPAD]
        target = moved_state.at[c] if c < NV else moved_adjoint.at[c - NV]
        put(columns.at[c], target)
    rest = recv[:, COLS * CAP : BLOCK, :].reshape(GRP * 8, MPAD)
    parts = [rest] + [pltpu.roll(rest, MPAD - REST * n, 1) for n in (1, 2)]
    parts = [part.reshape(GRP, 1, 8, MPAD) for part in parts]
    lines = jnp.concatenate(parts, axis=1).reshape(SLOTS, MPAD).T
    rows = [spare[c, 0:SPARE, :] for c in range(COLS)]
    whole = jnp.concatenate(rows + [lines[REST_AT : REST_AT + REST]], axis=0)
    for i in range(P1):
        for j in range(P1):
            at = (i * P1 + j) * 3
            factors[i, j] = whole[at : at + 3]
    put(factors, moved_factors)
    order[...] = whole[FROWS - 1 : FROWS].astype(jnp.int32).reshape(SLOTS)
    put(order, moved_order)
    for copy in copies:
        copy.wait()


def body(state, adjoint, factors, order, marks, neighbours, new_owner):
    vol_u, vol_p, face_u, face_p, tangents = [jnp.asarray(t) for t in tables()]
    hbm = pl.BlockSpec(memory_space=pltpu.HBM)
    vmem = pl.BlockSpec(memory_space=pltpu.VMEM)
    dma = pltpu.SemaphoreType.DMA
    copies = GRP - 1 + 2 * NEAR * (len(PIECES) - 1)
    arrays = (
        state,
        adjoint,
        factors.transpose(1, 2, 0, 3),
        order.reshape(1, ELEM),
        marks.reshape(1, ELEM),
        neighbours,
        new_owner.reshape(1, ELEM),
        vol_u,
        vol_p,
        face_u,
        face_p,
        tangents,
    )
    recv, share = pl.pallas_call(
        work,
        name="indicator_and_send",
        out_shape=(
            pltpu.VMEM((GRP, BLOCK, MPAD), F32),
            pltpu.VMEM((1, ELEM), F32),
        ),
        in_specs=[hbm] * len(arrays),
        out_specs=(vmem, vmem),
        scratch_shapes=[
            pltpu.VMEM((1, ELEM), jnp.int32),
            pltpu.VMEM((1, ELEM), jnp.int32),
            pltpu.VMEM((1, ELEM), jnp.int32),
            pltpu.VMEM((NV, MODES, ELEM), F32),
            pltpu.VMEM((P1, P1, 3, ELEM), F32),
            pltpu.VMEM((NV, MODES, ELEM), F32),
            pltpu.VMEM((6, ELEM), jnp.int32),
            pltpu.VMEM(tangents.shape, BF16),
            pltpu.VMEM(vol_u.shape, BF16),
            pltpu.VMEM(vol_p.shape, BF16),
            pltpu.VMEM(face_u.shape, BF16),
            pltpu.VMEM(face_p.shape, BF16),
            pltpu.VMEM((GRP, BLOCK, MPAD), F32),
            pltpu.VMEM((SLOTS, ELEM), BF16),
            pltpu.VMEM((MPAD, ELEM), jnp.int32),
            pltpu.VMEM((MPAD, ELEM), F32),
            pltpu.VMEM((80, ELEM), F32),
            pltpu.VMEM((2 * NV, 8, ELEM), F32),
            pltpu.VMEM((NV, KCAT, ELEM), BF16),
            pltpu.VMEM((NV, KCAT, ELEM), BF16),
            pltpu.VMEM((2, NV * TM, ELEM), F32),
            pltpu.VMEM((6, NV * TM, ELEM), F32),
            pltpu.VMEM((6, NV, PT, ELEM), F32),
            pltpu.VMEM((6, NV, PT, ELEM), F32),
            pltpu.VMEM((NV, 4 * PT, ELEM), F32),
            pltpu.VMEM((NV, 176, ELEM), F32),
            pltpu.VMEM((8, ELEM), F32),
            pltpu.VMEM((3 * TM, NV * ELEM), BF16),
            pltpu.VMEM((LEAF, 8, 128), F32),
            pltpu.VMEM((ROWS, 8, 128), F32),
            pltpu.VMEM((GRP, 8, 128), F32),
            dma((12,)),
            dma,
            dma((copies,)),
            dma((copies,)),
            dma((2,)),
            dma((2,)),
            dma((LEAF,)),
            dma((LEAF,)),
            dma((ROWS,)),
            dma((ROWS,)),
            dma((GRP,)),
            dma((GRP,)),
            pltpu.SemaphoreType.REGULAR((3,)),
            pltpu.SemaphoreType.REGULAR((4,)),
        ],
        compiler_params=pltpu.CompilerParams(
            collective_id=0, has_side_effects=True, vmem_limit_bytes=32 << 20
        ),
    )(*[pltpu.with_memory_space_constraint(x, pltpu.HBM) for x in arrays])
    moved_state, moved_adjoint, moved_factors, moved_order, share = pl.pallas_call(
        unpack,
        name="unpack_slots",
        out_shape=(
            jax.ShapeDtypeStruct((NV, MODES, SLOTS), F32),
            jax.ShapeDtypeStruct((NV, MODES, SLOTS), F32),
            jax.ShapeDtypeStruct((P1, P1, 3, SLOTS), F32),
            jax.ShapeDtypeStruct((SLOTS,), jnp.int32),
            jax.ShapeDtypeStruct((1, ELEM), F32),
        ),
        in_specs=[vmem, vmem],
        out_specs=(hbm,) * 5,
        scratch_shapes=[
            pltpu.VMEM((COLS, MODES, SLOTS), F32),
            pltpu.VMEM((COLS, 8, SLOTS), F32),
            pltpu.VMEM((P1, P1, 3, SLOTS), F32),
            pltpu.VMEM((SLOTS,), jnp.int32),
            dma((COLS + 3,)),
        ],
        compiler_params=pltpu.CompilerParams(vmem_limit_bytes=24 << 20),
    )(*[pltpu.with_memory_space_constraint(x, pltpu.VMEM) for x in (recv, share)])
    return (
        share.reshape(ELEM),
        moved_state,
        moved_adjoint,
        moved_factors.transpose(2, 0, 1, 3),
        moved_order,
    )


def solution(mesh):
    return jax.shard_map(
        body,
        mesh=mesh,
        in_specs=(
            P(None, None, ("grp", "dom")),
            P(None, None, ("grp", "dom")),
            P(None, None, None, ("grp", "dom")),
            P(("grp", "dom")),
            P(("grp", "dom")),
            P(None, ("grp", "dom")),
            P(("grp", "dom"), None),
        ),
        out_specs=(
            P(("grp", "dom")),
            P(None, None, ("grp", "dom")),
            P(None, None, ("grp", "dom")),
            P(None, None, None, ("grp", "dom")),
            P(("grp", "dom")),
        ),
        check_vma=False,
    )
```
